128 devices in a mesh: row: 16 (over x_lo, z, core), col: 8 (over x_hi, y).
Axes of the slice: x: 4 (x_hi: 2, x_lo: 2; x = x_hi * 2 + x_lo), y: 4, z: 4, core: 2. Of those that a mesh axis runs over, the one named last changes fastest.
Arguments:
- hidden: bfloat16 [2048, 2560], P('row'), may hold values from -4 to 4
- rel_bins: int32 [2048, 2048], P('row', 'col'), may hold values from 0 to 64, as said below
- attn_gain: float32 [2560], replicated, may hold values from 0.25 to 1.75
- w_query: bfloat16 [2560, 2560], P(None, 'col'), may hold values from -0.25 to 0.25
- w_key: bfloat16 [2560, 2560], P(None, 'col'), may hold values from -0.25 to 0.25
- w_value: bfloat16 [2560, 2560], P(None, 'col'), may hold values from -0.125 to 0.125
- w_out: bfloat16 [2560, 2560], P('col'), may hold values from -0.125 to 0.125
- final_gain: float32 [2560], P('col'), may hold values from 0.25 to 1.75
- w_single: bfloat16 [2560, 1024], P('col'), may hold values from -0.125 to 0.125
- w_second: bfloat16 [1024, 1024], replicated, may hold values from -0.1875 to 0.1875
- w_left: bfloat16 [1024, 128], replicated, may hold values from -0.1875 to 0.1875
- w_right: bfloat16 [1024, 128], replicated, may hold values from -0.1875 to 0.1875
- rel_table: bfloat16 [65, 128], replicated, may hold values from -6 to 6
- pair_gain: float32 [128], replicated, may hold values from 0.25 to 1.75
- w_expand: bfloat16 [128, 512], replicated, may hold values from -0.5 to 0.5
- w_contract: bfloat16 [512, 128], replicated, may hold values from -0.25 to 0.25
Outputs:
- pair_rep: bfloat16 [2048, 2048, 128], P('row', 'col')
The draws below stay inside these ranges and needn't reach their ends.
Inputs may be any that keep to these rules, and one draw needn't show every extreme that they name: rel_bins[i, j] is the difference of the residue numbers of j and i, clipped to plus or minus (64) // 2 and shifted by (64) // 2.
All inputs are finite; a program needn't handle non-finite values.
Results may differ from the reference program's by a relative error of at most 0.013.
Values may be sent and summed in bfloat16 or wider, within the bound.
No kernel may reach another device: no remote copies, remote signals or barrier semaphores. Data moves between devices by JAX's collectives and lax.ppermute only.
A program may use at most 128 MiB of HBM per device.

```python
import math
import jax
import jax.numpy as jnp
from jax import lax

D = 2560
H = 40
HD = 64
CS = 1024
CZ = 128
CH = 512
NB = 65
L = 2048


def draw_hidden(key, part):
    place = jnp.arange(D, dtype=jnp.float32) / (D - 1)
    base = jnp.clip(jax.random.normal(key, (L, D), jnp.float32), -3.0, 3.0)
    result = base * (4.0 / 9.0) * 3.0 ** place[None, :]
    return result.astype(jnp.bfloat16)


def draw_rel_bins(key, part):
    first_key, second_key = jax.random.split(jax.random.fold_in(key, 17), 2)
    breaks = jax.random.randint(first_key, (L,), 0, 48, dtype=jnp.int32) == 0
    jumps = jax.random.randint(second_key, (L,), 1, 200, dtype=jnp.int32)
    strides = 1 + jnp.where(breaks, jumps, 0)
    numbers = jnp.cumsum(strides).astype(jnp.int32)
    reach = (NB - 1) // 2
    difference = numbers[None, :] - numbers[:, None]
    return (jnp.clip(difference, -reach, reach) + reach).astype(jnp.int32)


def level_of(stream_key, dims, shards, low, top_value):
    def one(position, shards_of):
        steps = jax.random.uniform(jax.random.fold_in(jax.random.fold_in(stream_key, 6), position), (shards_of,), jnp.float32, low / len(shards), top_value / len(shards))
        return jnp.repeat(jnp.exp(steps), dims[position] // shards_of).reshape((-1,) + (1,) * (len(dims) - position - 1))

    level = one(*shards[0])
    for cut in shards[1:]:
        level = level * one(*cut)
    return level


def centred(key, dims, spread, limit, cuts=(), kind=jnp.bfloat16):
    values = spread * jax.random.normal(key, dims, jnp.float32)
    if cuts:
        values = values * level_of(key, dims, cuts, -0.22, 0.18)
    return jnp.clip(values, -limit, limit).astype(kind)


def setup_inputs(seed: int = 0) -> dict:
    key_list = jax.random.split(jax.random.key(seed), 17)
    hidden = draw_hidden(jax.random.fold_in(key_list[16], 71), 0)
    rel_bins = draw_rel_bins(jax.random.fold_in(key_list[16], 71), 0)
    attn_gain = jnp.clip(1.0 + 0.15 * jax.random.normal(key_list[2], (D,), jnp.float32), 0.25, 1.75)
    w_query = centred(key_list[3], (D, D), (D // 4) ** -0.5, 0.25, ((1, 8),))
    w_key = centred(key_list[4], (D, D), (D // 4) ** -0.5, 0.25, ((1, 8),))
    w_value = centred(key_list[5], (D, D), D ** -0.5, 0.125, ((1, 8),))
    w_out = centred(key_list[6], (D, D), D ** -0.5, 0.125, ((0, 8),))
    final_gain = jnp.clip(1.0 + 0.15 * jax.random.normal(key_list[7], (D,), jnp.float32), 0.25, 1.75)
    w_single = centred(key_list[8], (D, CS), D ** -0.5, 0.125, ((0, 8),))
    w_second = centred(key_list[9], (CS, CS), CS ** -0.5, 0.1875)
    w_left = centred(key_list[10], (CS, CZ), CS ** -0.5, 0.1875)
    w_right = centred(key_list[11], (CS, CZ), CS ** -0.5, 0.1875)
    rel_table = centred(key_list[12], (NB, CZ), 1.0, 6.0)
    pair_gain = jnp.clip(1.0 + 0.15 * jax.random.normal(key_list[13], (CZ,), jnp.float32), 0.25, 1.75)
    w_expand = centred(key_list[14], (CZ, CH), CZ ** -0.5, 0.5)
    w_contract = centred(key_list[15], (CH, CZ), CH ** -0.5, 0.25)
    return dict(hidden=hidden, rel_bins=rel_bins, attn_gain=attn_gain, w_query=w_query, w_key=w_key, w_value=w_value, w_out=w_out, final_gain=final_gain, w_single=w_single, w_second=w_second, w_left=w_left, w_right=w_right, rel_table=rel_table, pair_gain=pair_gain, w_expand=w_expand, w_contract=w_contract)


epsilon = 1e-05

def layer_norm(values, gain):
    count = values.shape[-1]
    average = lax.optimization_barrier(jnp.sum(values, -1, keepdims=True)) / count
    variance = lax.optimization_barrier(jnp.sum(values * values, -1, keepdims=True)) / count - average * average
    return (values - average) * lax.rsqrt(variance + epsilon) * gain

def rotary(vectors, positions):
    half_size = vectors.shape[-1] // 2
    frequency = jnp.exp(jnp.arange(half_size, dtype=jnp.float32) * (-2.0 * math.log(10000.0) / vectors.shape[-1]))
    angles = positions.astype(jnp.float32)[:, None] * frequency[None, :]
    angles = jnp.concatenate([angles, angles], -1)[:, None, :]
    turned = jnp.concatenate([-vectors[..., half_size:], vectors[..., :half_size]], -1)
    return vectors * jnp.cos(angles) + turned * jnp.sin(angles)

def one_head(entries):
    query_head, key_head, value_head = entries
    scores = jnp.dot(query_head, key_head.T, preferred_element_type=jnp.float32)
    weights = jnp.exp(scores)
    totals = lax.optimization_barrier(jnp.sum(weights, -1, keepdims=True))
    numerator = jnp.dot(weights.astype(jnp.bfloat16), value_head, preferred_element_type=jnp.float32)
    return (numerator / totals).astype(jnp.bfloat16)

def reference(hidden, rel_bins, attn_gain, w_query, w_key, w_value, w_out, final_gain, w_single, w_second, w_left, w_right, rel_table, pair_gain, w_expand, w_contract):
    residues = hidden.shape[0]
    positions = jnp.arange(residues, dtype=jnp.int32)
    stream = hidden.astype(jnp.float32)
    attn_in = layer_norm(stream, attn_gain).astype(jnp.bfloat16)
    query = jnp.dot(attn_in, w_query, preferred_element_type=jnp.float32) * HD ** (-0.5)
    query = rotary(query.reshape(residues, H, HD), positions).astype(jnp.bfloat16)
    keys = jnp.dot(attn_in, w_key, preferred_element_type=jnp.float32)
    keys = rotary(keys.reshape(residues, H, HD), positions).astype(jnp.bfloat16)
    values = jnp.dot(attn_in, w_value, preferred_element_type=jnp.float32).astype(jnp.bfloat16).reshape(residues, H, HD)
    context = lax.map(one_head, (jnp.transpose(query, (1, 0, 2)), jnp.transpose(keys, (1, 0, 2)), jnp.transpose(values, (1, 0, 2))))
    context = jnp.transpose(context, (1, 0, 2)).reshape(residues, H * HD)
    resid = stream + jnp.dot(context, w_out, preferred_element_type=jnp.float32)
    final = layer_norm(resid, final_gain).astype(jnp.bfloat16)
    lifted = jnp.maximum(jnp.dot(final, w_single, preferred_element_type=jnp.float32), 0.0).astype(jnp.bfloat16)
    single = jnp.dot(lifted, w_second, preferred_element_type=jnp.float32).astype(jnp.bfloat16)
    left = jnp.dot(single, w_left, preferred_element_type=jnp.float32).astype(jnp.bfloat16)
    right = jnp.dot(single, w_right, preferred_element_type=jnp.float32).astype(jnp.bfloat16)
    left_wide = left.astype(jnp.float32)
    right_wide = right.astype(jnp.float32)
    block_rows = math.gcd(residues, 128)

    def pair_tile(entries):
        bin_block, left_block = entries
        pair_in = left_block[:, None, :] + right_wide[None, :, :] + jnp.take(rel_table, bin_block, axis=0).astype(jnp.float32)
        normed = layer_norm(pair_in, pair_gain).astype(jnp.bfloat16)
        flat = normed.reshape(-1, normed.shape[-1])
        expanded = jnp.maximum(jnp.dot(flat, w_expand, preferred_element_type=jnp.float32), 0.0).astype(jnp.bfloat16)
        update = jnp.dot(expanded, w_contract, preferred_element_type=jnp.float32).reshape(pair_in.shape)
        return (pair_in + update).astype(jnp.bfloat16)
    pair_rep = lax.map(pair_tile, (rel_bins.reshape(residues // block_rows, block_rows, residues), left_wide.reshape(residues // block_rows, block_rows, -1)))
    return pair_rep.reshape(residues, residues, -1)
```

```python
import math

import jax
import jax.numpy as jnp
from jax import lax
from jax.sharding import PartitionSpec as P

HD = 64


epsilon = 1e-05


def layer_norm(values, gain):
    count = values.shape[-1]
    average = jnp.sum(values, -1, keepdims=True) / count
    variance = jnp.sum(values * values, -1, keepdims=True) / count - average * average
    return (values - average) * lax.rsqrt(variance + epsilon) * gain


def rotary(vectors, positions):
    half_size = vectors.shape[-1] // 2
    frequency = jnp.exp(
        jnp.arange(half_size, dtype=jnp.float32) * (-2.0 * math.log(10000.0) / vectors.shape[-1])
    )
    angles = positions.astype(jnp.float32)[:, None] * frequency[None, :]
    angles = jnp.concatenate([angles, angles], -1)[:, None, :]
    turned = jnp.concatenate([-vectors[..., half_size:], vectors[..., :half_size]], -1)
    return vectors * jnp.cos(angles) + turned * jnp.sin(angles)


def flip_pairs(size, bit):
    return [(place, place ^ bit) for place in range(size)]


def along_z(step):
    return [(place, place // 8 * 8 + (place % 8 + 2 * step) % 8) for place in range(16)]


def along_y(step):
    return [(place, place // 4 * 4 + (place + step) % 4) for place in range(8)]


def right_pairs(flip):
    return [
        ((2 * col + ((row // 8) ^ flip)) * 8 + row % 8, row * 8 + col)
        for row in range(16)
        for col in range(8)
    ]


def local(
    hidden,
    rel_bins,
    attn_gain,
    w_query,
    w_key,
    w_value,
    w_out,
    final_gain,
    w_single,
    w_second,
    w_left,
    w_right,
    rel_table,
    pair_gain,
    w_expand,
    w_contract,
):
    row_count = hidden.shape[0]
    model_width = hidden.shape[1]
    local_width = w_query.shape[1]
    local_heads = local_width // HD
    positions = lax.axis_index("row") * row_count + jnp.arange(row_count, dtype=jnp.int32)
    stream = hidden.astype(jnp.float32)
    attn_in = layer_norm(stream, attn_gain).astype(jnp.bfloat16)
    query = jnp.dot(attn_in, w_query, preferred_element_type=jnp.float32) * HD ** (-0.5)
    query = rotary(query.reshape(row_count, local_heads, HD), positions).astype(jnp.bfloat16)
    keys = jnp.dot(attn_in, w_key, preferred_element_type=jnp.float32)
    keys = rotary(keys.reshape(row_count, local_heads, HD), positions).astype(jnp.bfloat16)
    values = jnp.dot(attn_in, w_value, preferred_element_type=jnp.float32).astype(jnp.bfloat16)
    stacked = jnp.concatenate([keys.reshape(row_count, local_width), values], 1)
    query = query.reshape(row_count, local_width)

    blocks = [stacked] + [lax.ppermute(stacked, "row", along_z(step)) for step in (1, 3, 2)]
    other_query = lax.ppermute(query, "row", flip_pairs(16, 8))
    own_half = jnp.concatenate(blocks, 0)
    other_half = lax.ppermute(own_half, "row", flip_pairs(16, 1))
    incoming = jnp.concatenate([own_half, other_half], 0)
    both_query = jnp.concatenate([query, other_query], 0).reshape(-1, local_heads, HD)

    core = lax.rem(lax.axis_index("row"), 2)
    col_index = lax.axis_index("col")
    half_columns = w_single.shape[1] // 2
    own_part = lax.dynamic_slice_in_dim(w_single, core * half_columns, half_columns, 1)
    own_part = (own_part.astype(jnp.float32) * final_gain[:, None]).astype(jnp.bfloat16)
    quarter = [own_part] + [lax.ppermute(own_part, "col", along_y(step)) for step in (1, 3, 2)]
    quarter = jnp.concatenate(quarter, 0)
    gathered = jnp.concatenate([quarter, lax.ppermute(quarter, "col", flip_pairs(8, 4))], 0)
    gathered_other = lax.ppermute(gathered, "row", flip_pairs(16, 1))

    key_block = incoming[:, :local_width].reshape(-1, local_heads, HD)
    value_block = incoming[:, local_width:].reshape(-1, local_heads, HD)
    scores = jnp.einsum("qhd,khd->hqk", both_query, key_block, preferred_element_type=jnp.float32)
    weights = jnp.exp(scores)
    totals = jnp.sum(weights, -1)
    numerator = jnp.einsum(
        "hqk,khd->hqd",
        weights.astype(jnp.bfloat16),
        value_block,
        preferred_element_type=jnp.float32,
    )
    sent = numerator[:, row_count:].astype(jnp.bfloat16)
    numerator = numerator[:, :row_count] + lax.ppermute(sent, "row", flip_pairs(16, 8)).astype(
        jnp.float32
    )
    totals = totals[:, :row_count] + lax.ppermute(totals[:, row_count:], "row", flip_pairs(16, 8))
    context = (numerator / totals[..., None]).astype(jnp.bfloat16)
    context = jnp.transpose(context, (1, 0, 2)).reshape(row_count, local_width)
    attn_part = jnp.dot(context, w_out, preferred_element_type=jnp.float32).astype(jnp.bfloat16)

    col_size = lax.axis_size("col")
    own_count = row_count // col_size
    parts = lax.all_to_all(
        attn_part.reshape(col_size, own_count, model_width), "col", 0, 0, tiled=False
    )
    own_stream = lax.dynamic_slice_in_dim(stream, col_index * own_count, own_count, 0)
    resid = own_stream + jnp.sum(parts.astype(jnp.float32), 0)
    final = layer_norm(resid, 1.0).astype(jnp.bfloat16)
    far, near = (col_index // 4) * 4, lax.rem(col_index, 4)
    order = [far + lax.rem(near + shift, 4) for shift in (0, 3, 1, 2)]
    order = order + [lax.rem(place + 4, 8) for place in order]
    final = jnp.concatenate(
        [lax.dynamic_slice_in_dim(final, place * local_width, local_width, 1) for place in order], 1
    )
    lifted = []
    for block in (gathered, gathered_other):
        summed = jnp.dot(final, block, preferred_element_type=jnp.float32)
        lifted.append(jnp.maximum(summed, 0.0).astype(jnp.bfloat16))
    single = sum(
        jnp.dot(
            part,
            lax.dynamic_slice_in_dim(w_second, side * half_columns, half_columns, 0),
            preferred_element_type=jnp.float32,
        )
        for part, side in zip(lifted, (core, 1 - core))
    ).astype(jnp.bfloat16)
    both = jnp.concatenate([w_left, w_right], 1)
    both = jnp.dot(single, both, preferred_element_type=jnp.float32).astype(jnp.bfloat16)
    both = lax.all_to_all(
        jnp.broadcast_to(both, (col_size,) + both.shape), "col", 0, 0, tiled=False
    ).reshape(row_count, -1)
    channels = w_left.shape[1]
    left, right = both[:, :channels], both[:, channels:]
    first = lax.ppermute(right, ("row", "col"), right_pairs(0))
    second = lax.ppermute(right, ("row", "col"), right_pairs(1))
    upper = lax.axis_index("row") < 8
    column_right = jnp.concatenate(
        [jnp.where(upper, first, second), jnp.where(upper, second, first)], 0
    )
    col_count = column_right.shape[0]
    channels = column_right.shape[1]
    right_wide = column_right.astype(jnp.float32)
    left_wide = left.astype(jnp.float32)
    block_rows = math.gcd(row_count, 32)
    bin_codes = jnp.arange(rel_table.shape[0], dtype=jnp.int32)

    def pair_tile(entries):
        bin_block, left_block = entries
        one_hot = (bin_block[..., None] == bin_codes).astype(jnp.bfloat16)
        table_part = jnp.einsum(
            "ijb,bc->ijc", one_hot, rel_table, preferred_element_type=jnp.float32
        )
        pair_in = left_block[:, None, :] + right_wide[None, :, :] + table_part
        normed = layer_norm(pair_in, pair_gain).astype(jnp.bfloat16)
        flat = normed.reshape(-1, channels)
        expanded = jnp.maximum(
            jnp.dot(flat, w_expand, preferred_element_type=jnp.float32), 0.0
        ).astype(jnp.bfloat16)
        update = jnp.dot(expanded, w_contract, preferred_element_type=jnp.float32).reshape(
            pair_in.shape
        )
        return (pair_in + update).astype(jnp.bfloat16)

    pair_rep = lax.map(
        pair_tile,
        (
            rel_bins.reshape(row_count // block_rows, block_rows, col_count),
            left_wide.reshape(row_count // block_rows, block_rows, channels),
        ),
    )
    return pair_rep.reshape(row_count, col_count, channels)


def solution(mesh):
    in_specs = (
        P("row", None),
        P("row", "col"),
        P(),
        P(None, "col"),
        P(None, "col"),
        P(None, "col"),
        P("col", None),
        P("col"),
        P("col", None),
        P(),
        P(),
        P(),
        P(),
        P(),
        P(),
        P(),
    )
    out_specs = P("row", "col", None)
    return jax.shard_map(local, mesh=mesh, in_specs=in_specs, out_specs=out_specs, check_vma=False)
```

```python
import math

import jax
import jax.numpy as jnp
from jax import lax
from jax.experimental import pallas as pl
from jax.experimental.pallas import tpu as pltpu
from jax.sharding import PartitionSpec as P

HD = 64


epsilon = 1e-05


def layer_norm(values, gain):
    count = values.shape[-1]
    average = jnp.sum(values, -1, keepdims=True) / count
    variance = jnp.sum(values * values, -1, keepdims=True) / count - average * average
    return (values - average) * lax.rsqrt(variance + epsilon) * gain


def rotary(vectors, positions):
    half_size = vectors.shape[-1] // 2
    frequency = jnp.exp(
        jnp.arange(half_size, dtype=jnp.float32) * (-2.0 * math.log(10000.0) / vectors.shape[-1])
    )
    angles = positions.astype(jnp.float32)[:, None] * frequency[None, :]
    angles = jnp.concatenate([angles, angles], -1)[:, None, :]
    turned = jnp.concatenate([-vectors[..., half_size:], vectors[..., :half_size]], -1)
    return vectors * jnp.cos(angles) + turned * jnp.sin(angles)


def flip_pairs(size, bit):
    return [(place, place ^ bit) for place in range(size)]


def along_z(step):
    return [(place, place // 8 * 8 + (place % 8 + 2 * step) % 8) for place in range(16)]


def along_y(step):
    return [(place, place // 4 * 4 + (place + step) % 4) for place in range(8)]


def right_pairs(flip):
    return [
        ((2 * col + ((row // 8) ^ flip)) * 8 + row % 8, row * 8 + col)
        for row in range(16)
        for col in range(8)
    ]


def whole(array):
    return pl.BlockSpec(array.shape, lambda step: (0,) * array.ndim)


def pair_kernel(table_ref, left_ref, right_ref, gain_ref, expand_ref, contract_ref, out_ref):
    rows, columns, channels = table_ref.shape
    group = 8

    def pair_in(part):
        sums = left_ref[part, :][:, None, :] + right_ref[...][None]
        return table_ref[part].astype(jnp.float32) + sums

    for start in range(0, rows, group):
        part = slice(start, start + group)
        normed = layer_norm(pair_in(part), gain_ref[...]).astype(jnp.bfloat16)
        expanded = jnp.dot(
            normed.reshape(group * columns, channels),
            expand_ref[...],
            preferred_element_type=jnp.float32,
        )
        expanded = jnp.maximum(expanded.astype(jnp.bfloat16), 0)
        update = jnp.dot(expanded, contract_ref[...], preferred_element_type=jnp.float32)
        out_ref[part] = (pair_in(part) + update.reshape(group, columns, channels)).astype(
            jnp.bfloat16
        )


def pair_stage(table_part, left, right, gain, w_expand, w_contract):
    rows, columns, channels = table_part.shape
    block = 16
    left = left.astype(jnp.float32)
    right = right.astype(jnp.float32)
    gain = gain.reshape(1, channels)
    fixed = [right, gain, w_expand, w_contract]
    return pl.pallas_call(
        pair_kernel,
        grid=(rows // block,),
        in_specs=[
            pl.BlockSpec((block, columns, channels), lambda step: (step, 0, 0)),
            pl.BlockSpec((block, channels), lambda step: (step, 0)),
        ]
        + [whole(array) for array in fixed],
        out_specs=pl.BlockSpec((block, columns, channels), lambda step: (step, 0, 0)),
        out_shape=jax.ShapeDtypeStruct(table_part.shape, jnp.bfloat16),
        compiler_params=pltpu.CompilerParams(vmem_limit_bytes=48 << 20),
        name="pair",
    )(table_part, left, *fixed)


def local(
    hidden,
    rel_bins,
    attn_gain,
    w_query,
    w_key,
    w_value,
    w_out,
    final_gain,
    w_single,
    w_second,
    w_left,
    w_right,
    rel_table,
    pair_gain,
    w_expand,
    w_contract,
):
    row_count = hidden.shape[0]
    model_width = hidden.shape[1]
    local_width = w_query.shape[1]
    local_heads = local_width // HD
    positions = lax.axis_index("row") * row_count + jnp.arange(row_count, dtype=jnp.int32)
    stream = hidden.astype(jnp.float32)
    attn_in = layer_norm(stream, attn_gain).astype(jnp.bfloat16)
    keys = jnp.dot(attn_in, w_key, preferred_element_type=jnp.float32)
    keys = rotary(keys.reshape(row_count, local_heads, HD), positions).astype(jnp.bfloat16)
    values = jnp.dot(attn_in, w_value, preferred_element_type=jnp.float32).astype(jnp.bfloat16)
    stacked = jnp.concatenate([keys.reshape(row_count, local_width), values], 1)
    stacked, attn_in = lax.optimization_barrier((stacked, attn_in))

    blocks = [stacked] + [lax.ppermute(stacked, "row", along_z(step)) for step in (1, 3, 2)]
    query = jnp.dot(attn_in, w_query, preferred_element_type=jnp.float32) * HD ** (-0.5)
    query = rotary(query.reshape(row_count, local_heads, HD), positions).astype(jnp.bfloat16)
    query = query.reshape(row_count, local_width)
    query, w_single, rel_bins = lax.optimization_barrier((query, w_single, rel_bins))
    other_query = lax.ppermute(query, "row", flip_pairs(16, 8))

    core = lax.rem(lax.axis_index("row"), 2)
    col_index = lax.axis_index("col")
    half_columns = w_single.shape[1] // 2
    own_part = lax.dynamic_slice_in_dim(w_single, core * half_columns, half_columns, 1)
    own_part = (own_part.astype(jnp.float32) * final_gain[:, None]).astype(jnp.bfloat16)
    quarter = [own_part] + [lax.ppermute(own_part, "col", along_y(step)) for step in (1, 3, 2)]
    quarter = jnp.concatenate(quarter, 0)
    quarter_other = lax.ppermute(quarter, "row", flip_pairs(16, 1))

    bin_codes = jnp.arange(rel_table.shape[0], dtype=jnp.int32)
    one_hot = (rel_bins[..., None] == bin_codes).astype(jnp.bfloat16)
    table_part = jnp.einsum(
        "ijb,bc->ijc", one_hot, rel_table, preferred_element_type=jnp.float32
    ).astype(jnp.bfloat16)

    own_half = jnp.concatenate(blocks, 0)
    other_half = lax.ppermute(own_half, "row", flip_pairs(16, 1))
    incoming = jnp.concatenate([own_half, other_half], 0)
    both_query = jnp.concatenate([query, other_query], 0).reshape(-1, local_heads, HD)
    key_block = incoming[:, :local_width].reshape(-1, local_heads, HD)
    value_block = incoming[:, local_width:].reshape(-1, local_heads, HD)
    scores = jnp.einsum("qhd,khd->hqk", both_query, key_block, preferred_element_type=jnp.float32)
    weights = jnp.exp(scores)
    totals = jnp.sum(weights, -1)
    numerator = jnp.einsum(
        "hqk,khd->hqd",
        weights.astype(jnp.bfloat16),
        value_block,
        preferred_element_type=jnp.float32,
    )
    sent = jnp.concatenate([numerator, jnp.broadcast_to(totals[..., None], numerator.shape)], -1)
    received = lax.ppermute(sent[:, row_count:], "row", flip_pairs(16, 8))
    combined = sent[:, :row_count] + received
    context = (combined[..., :HD] / combined[..., HD:]).astype(jnp.bfloat16)
    context = jnp.transpose(context, (1, 0, 2)).reshape(row_count, local_width)
    half_width = model_width // 2
    attn_part = jnp.einsum(
        "rk,kxn->xrn",
        context,
        w_out.reshape(local_width, 2, half_width),
        preferred_element_type=jnp.float32,
    ).astype(jnp.bfloat16)

    own_count = row_count // 4
    far, near = col_index // 4, lax.rem(col_index, 4)
    parts = lax.all_to_all(
        attn_part.reshape(8, own_count, half_width), "col", 0, 0, tiled=False
    )
    own_stream = lax.dynamic_slice(
        hidden, (near * own_count, far * half_width), (own_count, half_width)
    ).astype(jnp.float32)
    resid = own_stream + jnp.sum(parts.astype(jnp.float32), 0)
    average = jnp.sum(resid, -1, keepdims=True) / half_width
    centred = resid - average
    spread = jnp.sum(centred * centred, -1, keepdims=True)
    centred = centred.astype(jnp.bfloat16)
    centred = jnp.concatenate(
        [
            lax.dynamic_slice_in_dim(centred, lax.rem(near + shift, 4) * local_width, local_width, 1)
            for shift in (0, 3, 1, 2)
        ],
        1,
    )
    ones = jnp.ones((8, half_width), jnp.bfloat16)
    centred = jnp.concatenate([centred, ones], 0)
    mine = [
        jnp.dot(centred, block, preferred_element_type=jnp.float32)
        for block in (quarter, quarter_other)
    ]
    low = core == 0
    mine = jnp.concatenate(
        [jnp.where(low, mine[0], mine[1]), jnp.where(low, mine[1], mine[0])], 1
    )
    statistics = jnp.concatenate(
        [jnp.broadcast_to(average, (own_count, 64)), jnp.broadcast_to(spread, (own_count, 64))], 1
    )
    statistics = jnp.concatenate([statistics, jnp.zeros((8, 128), jnp.float32)], 0)
    mine = jnp.concatenate([mine, statistics], 1)
    theirs = lax.ppermute(mine, "col", flip_pairs(8, 4))
    width = half_columns * 2
    average, other_average = mine[:own_count, width : width + 1], theirs[:own_count, width : width + 1]
    spread = mine[:own_count, width + 64 : width + 65] + theirs[:own_count, width + 64 : width + 65]
    apart = 0.5 * (average - other_average)
    variance = (spread + model_width * apart * apart) / model_width
    column_sums = mine[own_count : own_count + 1, :width] - theirs[own_count : own_count + 1, :width]
    summed = mine[:own_count, :width] + theirs[:own_count, :width] + apart * column_sums
    lifted = jnp.maximum(summed * lax.rsqrt(variance + epsilon), 0.0).astype(jnp.bfloat16)
    single = jnp.dot(lifted, w_second, preferred_element_type=jnp.float32).astype(jnp.bfloat16)
    both = jnp.concatenate([w_left, w_right], 1)
    both = jnp.dot(single, both, preferred_element_type=jnp.float32).astype(jnp.bfloat16)
    both = lax.all_to_all(
        jnp.broadcast_to(both, (4,) + both.shape),
        "col",
        0,
        0,
        tiled=False,
        axis_index_groups=[[0, 1, 2, 3], [4, 5, 6, 7]],
    ).reshape(row_count, -1)
    channels = w_left.shape[1]
    left, right = both[:, :channels], both[:, channels:]
    first = lax.ppermute(right, ("row", "col"), right_pairs(0))
    second = lax.ppermute(right, ("row", "col"), right_pairs(1))
    upper = lax.axis_index("row") < 8
    column_right = jnp.concatenate(
        [jnp.where(upper, first, second), jnp.where(upper, second, first)], 0
    )
    return pair_stage(table_part, left, column_right, pair_gain, w_expand, w_contract)


def solution(mesh):
    in_specs = (
        P("row", None),
        P("row", "col"),
        P(),
        P(None, "col"),
        P(None, "col"),
        P(None, "col"),
        P("col", None),
        P("col"),
        P("col", None),
        P(),
        P(),
        P(),
        P(),
        P(),
        P(),
        P(),
    )
    out_specs = P("row", "col", None)
    return jax.shard_map(local, mesh=mesh, in_specs=in_specs, out_specs=out_specs, check_vma=False)
```

```python
import math

import jax
import jax.numpy as jnp
from jax import lax
from jax.experimental import pallas as pl
from jax.experimental.pallas import tpu as pltpu
from jax.sharding import PartitionSpec as P

HD = 64


epsilon = 1e-05


def layer_norm(values, gain):
    count = values.shape[-1]
    average = jnp.sum(values, -1, keepdims=True) / count
    variance = jnp.sum(values * values, -1, keepdims=True) / count - average * average
    return (values - average) * lax.rsqrt(variance + epsilon) * gain


def rotary(vectors, positions):
    half_size = vectors.shape[-1] // 2
    frequency = jnp.exp(
        jnp.arange(half_size, dtype=jnp.float32) * (-2.0 * math.log(10000.0) / vectors.shape[-1])
    )
    angles = positions.astype(jnp.float32)[:, None] * frequency[None, :]
    angles = jnp.concatenate([angles, angles], -1)[:, None, :]
    turned = jnp.concatenate([-vectors[..., half_size:], vectors[..., :half_size]], -1)
    return vectors * jnp.cos(angles) + turned * jnp.sin(angles)


def flip_pairs(size, bit):
    return [(place, place ^ bit) for place in range(size)]


def along_z(step):
    return [(place, place // 8 * 8 + (place % 8 + 2 * step) % 8) for place in range(16)]


def along_y(step):
    return [(place, place // 4 * 4 + (place + step) % 4) for place in range(8)]


def right_pairs(flip):
    return [
        ((2 * col + ((row // 8) ^ flip)) * 8 + row % 8, row * 8 + col)
        for row in range(16)
        for col in range(8)
    ]


def whole(array):
    return pl.BlockSpec(array.shape, lambda step: (0,) * array.ndim)


def pair_kernel(table_ref, left_ref, right_ref, gain_ref, expand_ref, contract_ref, out_ref):
    rows, columns, channels = table_ref.shape
    group = 8

    def pair_in(part):
        sums = left_ref[part, :][:, None, :] + right_ref[...][None]
        return table_ref[part].astype(jnp.float32) + sums

    for start in range(0, rows, group):
        part = slice(start, start + group)
        normed = layer_norm(pair_in(part), gain_ref[...]).astype(jnp.bfloat16)
        expanded = jnp.dot(
            normed.reshape(group * columns, channels),
            expand_ref[...],
            preferred_element_type=jnp.float32,
        )
        expanded = jnp.maximum(expanded.astype(jnp.bfloat16), 0)
        update = jnp.dot(expanded, contract_ref[...], preferred_element_type=jnp.float32)
        out_ref[part] = (pair_in(part) + update.reshape(group, columns, channels)).astype(
            jnp.bfloat16
        )


def pair_stage(table_part, left, right, gain, w_expand, w_contract):
    rows, columns, channels = table_part.shape
    block = 16
    left = left.astype(jnp.float32)
    right = right.astype(jnp.float32)
    gain = gain.reshape(1, channels)
    fixed = [right, gain, w_expand, w_contract]
    return pl.pallas_call(
        pair_kernel,
        grid=(rows // block,),
        in_specs=[
            pl.BlockSpec((block, columns, channels), lambda step: (step, 0, 0)),
            pl.BlockSpec((block, channels), lambda step: (step, 0)),
        ]
        + [whole(array) for array in fixed],
        out_specs=pl.BlockSpec((block, columns, channels), lambda step: (step, 0, 0)),
        out_shape=jax.ShapeDtypeStruct(table_part.shape, jnp.bfloat16),
        compiler_params=pltpu.CompilerParams(vmem_limit_bytes=48 << 20),
        name="pair",
    )(table_part, left, *fixed)


def half_sums_kernel(
    place_ref, parts_ref, stream_ref, own_ref, other_ref, mine_ref, sent_ref, blocks_ref
):
    near, core = place_ref[0], place_ref[2]
    rows, features = stream_ref.shape
    local_width = features // 4
    half_columns = own_ref.shape[1]
    resid = stream_ref[...].astype(jnp.float32)
    for part in range(parts_ref.shape[0]):
        resid += parts_ref[part].astype(jnp.float32)
    average = jnp.sum(resid, -1, keepdims=True) / features
    centred = resid - average
    spread = jnp.sum(centred * centred, -1, keepdims=True)
    centred = centred.astype(jnp.bfloat16)
    for block in range(4):
        blocks_ref[block, :rows, :] = centred[:, block * local_width : (block + 1) * local_width]
        blocks_ref[block, rows:, :] = jnp.ones((16, local_width), jnp.bfloat16)
    line = lax.broadcasted_iota(jnp.int32, (16, half_columns), 0)
    for ref, side in ((own_ref, core), (other_ref, 1 - core)):
        total = jnp.zeros((rows + 16, half_columns), jnp.float32)
        for position, shift in enumerate((0, 3, 1, 2)):
            total += jnp.dot(
                blocks_ref[lax.rem(near + shift, 4)],
                ref[position * local_width : (position + 1) * local_width, :],
                preferred_element_type=jnp.float32,
            )
        columns = pl.ds(pl.multiple_of(side * half_columns, half_columns), half_columns)
        mine_ref[:, columns] = total
        sums = total[rows:]
        high = sums.astype(jnp.bfloat16).astype(jnp.float32)
        sums = jnp.where(line == 0, high, jnp.where(line == 1, sums - high, 0.0))
        sent_ref[:rows, columns] = total[:rows].astype(jnp.bfloat16)
        sent_ref[rows:, columns] = sums.astype(jnp.bfloat16)
    lane = lax.broadcasted_iota(jnp.int32, (rows, 128), 1)
    width = half_columns * 2
    mine_ref[:rows, width:] = jnp.where(lane < 2, average, spread)
    mine_ref[rows:, width:] = jnp.zeros((16, 128), jnp.float32)
    high_average = average.astype(jnp.bfloat16).astype(jnp.float32)
    high_spread = spread.astype(jnp.bfloat16).astype(jnp.float32)
    terms = jnp.where(
        lane == 0,
        high_average,
        jnp.where(
            lane == 1,
            average - high_average,
            jnp.where(lane == 2, high_spread, spread - high_spread),
        ),
    )
    sent_ref[:rows, width:] = terms.astype(jnp.bfloat16)
    sent_ref[rows:, width:] = jnp.zeros((16, 128), jnp.bfloat16)


def half_sums(place, parts, hidden, own, other):
    rows, features = parts.shape[1:]
    width = own.shape[1] * 2 + 128

    def fixed(array):
        return pl.BlockSpec(array.shape, lambda step, place: (0,) * array.ndim)

    spec = pl.BlockSpec((rows + 16, width), lambda step, place: (0, 0))
    return pl.pallas_call(
        half_sums_kernel,
        grid_spec=pltpu.PrefetchScalarGridSpec(
            num_scalar_prefetch=1,
            grid=(1,),
            in_specs=[
                fixed(parts),
                pl.BlockSpec((rows, features), lambda step, place: (place[0], place[1])),
                fixed(own),
                fixed(other),
            ],
            out_specs=[spec, spec],
            scratch_shapes=[pltpu.VMEM((4, rows + 16, features // 4), jnp.bfloat16)],
        ),
        out_shape=[
            jax.ShapeDtypeStruct((rows + 16, width), jnp.float32),
            jax.ShapeDtypeStruct((rows + 16, width), jnp.bfloat16),
        ],
        compiler_params=pltpu.CompilerParams(vmem_limit_bytes=24 << 20),
        name="half_sums",
    )(place, parts, hidden, own, other)


def local(
    hidden,
    rel_bins,
    attn_gain,
    w_query,
    w_key,
    w_value,
    w_out,
    final_gain,
    w_single,
    w_second,
    w_left,
    w_right,
    rel_table,
    pair_gain,
    w_expand,
    w_contract,
):
    row_count = hidden.shape[0]
    model_width = hidden.shape[1]
    local_width = w_query.shape[1]
    local_heads = local_width // HD
    positions = lax.axis_index("row") * row_count + jnp.arange(row_count, dtype=jnp.int32)
    stream = hidden.astype(jnp.float32)
    attn_in = layer_norm(stream, attn_gain).astype(jnp.bfloat16)
    keys = jnp.dot(attn_in, w_key, preferred_element_type=jnp.float32)
    keys = rotary(keys.reshape(row_count, local_heads, HD), positions).astype(jnp.bfloat16)
    values = jnp.dot(attn_in, w_value, preferred_element_type=jnp.float32).astype(jnp.bfloat16)
    stacked = jnp.concatenate([keys.reshape(row_count, local_width), values], 1)
    stacked, attn_in = lax.optimization_barrier((stacked, attn_in))

    blocks = [stacked] + [lax.ppermute(stacked, "row", along_z(step)) for step in (1, 3, 2)]
    query = jnp.dot(attn_in, w_query, preferred_element_type=jnp.float32) * HD ** (-0.5)
    query = rotary(query.reshape(row_count, local_heads, HD), positions).astype(jnp.bfloat16)
    query = query.reshape(row_count, local_width)
    query, w_single, rel_bins = lax.optimization_barrier((query, w_single, rel_bins))
    other_query = lax.ppermute(query, "row", flip_pairs(16, 8))

    core = lax.rem(lax.axis_index("row"), 2)
    col_index = lax.axis_index("col")
    half_columns = w_single.shape[1] // 2
    own_part = lax.dynamic_slice_in_dim(w_single, core * half_columns, half_columns, 1)
    own_part = (own_part.astype(jnp.float32) * final_gain[:, None]).astype(jnp.bfloat16)
    quarter = [own_part] + [lax.ppermute(own_part, "col", along_y(step)) for step in (1, 3, 2)]
    quarter = jnp.concatenate(quarter, 0)
    quarter_other = lax.ppermute(quarter, "row", flip_pairs(16, 1))

    bin_codes = jnp.arange(rel_table.shape[0], dtype=jnp.int32)
    one_hot = (rel_bins[..., None] == bin_codes).astype(jnp.bfloat16)
    table_part = jnp.einsum(
        "ijb,bc->ijc", one_hot, rel_table, preferred_element_type=jnp.float32
    ).astype(jnp.bfloat16)

    own_half = jnp.concatenate(blocks, 0)
    other_half = lax.ppermute(own_half, "row", flip_pairs(16, 1))
    incoming = jnp.concatenate([own_half, other_half], 0)
    both_query = jnp.concatenate([query, other_query], 0).reshape(-1, local_heads, HD)
    key_block = incoming[:, :local_width].reshape(-1, local_heads, HD)
    value_block = incoming[:, local_width:].reshape(-1, local_heads, HD)
    scores = jnp.einsum("qhd,khd->hqk", both_query, key_block, preferred_element_type=jnp.float32)
    weights = jnp.exp(scores)
    totals = jnp.sum(weights, -1)
    numerator = jnp.einsum(
        "hqk,khd->hqd",
        weights.astype(jnp.bfloat16),
        value_block,
        preferred_element_type=jnp.float32,
    )
    sent_totals = jnp.transpose(totals[:, row_count:])
    high = lax.reduce_precision(sent_totals, 8, 7)
    sent = jnp.concatenate(
        [
            jnp.transpose(numerator[:, row_count:], (1, 0, 2)).reshape(row_count, local_width),
            jnp.pad(high, ((0, 0), (0, 32 - local_heads))),
            jnp.pad(sent_totals - high, ((0, 0), (0, 32 - local_heads))),
        ],
        1,
    ).astype(jnp.bfloat16)
    received = lax.ppermute(sent, "row", flip_pairs(16, 8)).astype(jnp.float32)
    other_totals = received[:, local_width : local_width + local_heads]
    other_totals += received[:, local_width + 32 : local_width + 32 + local_heads]
    totals = jnp.transpose(totals[:, :row_count]) + other_totals
    numerator = jnp.transpose(numerator[:, :row_count], (1, 0, 2))
    numerator += received[:, :local_width].reshape(row_count, local_heads, HD)
    context = (numerator / totals[..., None]).astype(jnp.bfloat16).reshape(row_count, local_width)
    half_width = model_width // 2
    attn_part = jnp.einsum(
        "rk,kxn->xrn",
        context,
        w_out.reshape(local_width, 2, half_width),
        preferred_element_type=jnp.float32,
    ).astype(jnp.bfloat16)

    own_count = row_count // 4
    far, near = col_index // 4, lax.rem(col_index, 4)
    parts = lax.all_to_all(
        attn_part.reshape(8, own_count, half_width), "col", 0, 0, tiled=False
    )
    parts, table_part = lax.optimization_barrier((parts, table_part))
    place = jnp.stack([near, far, core]).astype(jnp.int32)
    mine, sent = half_sums(place, parts, hidden, quarter, quarter_other)
    theirs = lax.ppermute(sent, "col", flip_pairs(8, 4)).astype(jnp.float32)
    width = half_columns * 2
    other_average = theirs[:own_count, width : width + 1] + theirs[:own_count, width + 1 : width + 2]
    other_spread = theirs[:own_count, width + 2 : width + 3] + theirs[:own_count, width + 3 : width + 4]
    average, spread = mine[:own_count, width : width + 1], mine[:own_count, width + 2 : width + 3]
    apart = 0.5 * (average - other_average)
    variance = (spread + other_spread + model_width * apart * apart) / model_width
    column_sums = mine[own_count : own_count + 1, :width] - (
        theirs[own_count : own_count + 1, :width] + theirs[own_count + 1 : own_count + 2, :width]
    )
    summed = mine[:own_count, :width] + theirs[:own_count, :width] + apart * column_sums
    lifted = jnp.maximum(summed * lax.rsqrt(variance + epsilon), 0.0).astype(jnp.bfloat16)
    single = jnp.dot(lifted, w_second, preferred_element_type=jnp.float32).astype(jnp.bfloat16)
    both = jnp.concatenate([w_left, w_right], 1)
    both = jnp.dot(single, both, preferred_element_type=jnp.float32).astype(jnp.bfloat16)
    both = lax.all_to_all(
        jnp.broadcast_to(both, (4,) + both.shape),
        "col",
        0,
        0,
        tiled=False,
        axis_index_groups=[[0, 1, 2, 3], [4, 5, 6, 7]],
    ).reshape(row_count, -1)
    channels = w_left.shape[1]
    left, right = both[:, :channels], both[:, channels:]
    first = lax.ppermute(right, ("row", "col"), right_pairs(0))
    second = lax.ppermute(right, ("row", "col"), right_pairs(1))
    upper = lax.axis_index("row") < 8
    column_right = jnp.concatenate(
        [jnp.where(upper, first, second), jnp.where(upper, second, first)], 0
    )
    return pair_stage(table_part, left, column_right, pair_gain, w_expand, w_contract)


def solution(mesh):
    in_specs = (
        P("row", None),
        P("row", "col"),
        P(),
        P(None, "col"),
        P(None, "col"),
        P(None, "col"),
        P("col", None),
        P("col"),
        P("col", None),
        P(),
        P(),
        P(),
        P(),
        P(),
        P(),
        P(),
    )
    out_specs = P("row", "col", None)
    return jax.shard_map(local, mesh=mesh, in_specs=in_specs, out_specs=out_specs, check_vma=False)
```

```python
import math

import jax
import jax.numpy as jnp
from jax import lax
from jax.experimental import pallas as pl
from jax.experimental.pallas import tpu as pltpu
from jax.sharding import PartitionSpec as P

HD = 64


epsilon = 1e-05


def layer_norm(values, gain):
    count = values.shape[-1]
    average = jnp.sum(values, -1, keepdims=True) / count
    variance = jnp.sum(values * values, -1, keepdims=True) / count - average * average
    return (values - average) * lax.rsqrt(variance + epsilon) * gain


def rotary(vectors, positions):
    half_size = vectors.shape[-1] // 2
    frequency = jnp.exp(
        jnp.arange(half_size, dtype=jnp.float32) * (-2.0 * math.log(10000.0) / vectors.shape[-1])
    )
    angles = positions.astype(jnp.float32)[:, None] * frequency[None, :]
    angles = jnp.concatenate([angles, angles], -1)[:, None, :]
    turned = jnp.concatenate([-vectors[..., half_size:], vectors[..., :half_size]], -1)
    return vectors * jnp.cos(angles) + turned * jnp.sin(angles)


def flip_pairs(size, bit):
    return [(place, place ^ bit) for place in range(size)]


def right_pairs(size, other_size):
    return [
        (row * other_size + col, (2 * col + row % 2) * other_size + row // 2)
        for row in range(size)
        for col in range(other_size)
    ]


def whole(array):
    return pl.BlockSpec(array.shape, lambda step: (0,) * array.ndim)


def pair_kernel(table_ref, left_ref, right_ref, gain_ref, expand_ref, contract_ref, out_ref):
    rows, columns, channels = table_ref.shape
    group = 8

    def pair_in(part):
        sums = left_ref[part, :][:, None, :] + right_ref[...][None]
        return table_ref[part].astype(jnp.float32) + sums

    for start in range(0, rows, group):
        part = slice(start, start + group)
        normed = layer_norm(pair_in(part), gain_ref[...]).astype(jnp.bfloat16)
        expanded = jnp.dot(
            normed.reshape(group * columns, channels),
            expand_ref[...],
            preferred_element_type=jnp.float32,
        )
        expanded = jnp.maximum(expanded.astype(jnp.bfloat16), 0)
        update = jnp.dot(expanded, contract_ref[...], preferred_element_type=jnp.float32)
        out_ref[part] = (pair_in(part) + update.reshape(group, columns, channels)).astype(
            jnp.bfloat16
        )


def pair_stage(table_part, left, right, gain, w_expand, w_contract):
    rows, columns, channels = table_part.shape
    block = 16
    left = left.astype(jnp.float32)
    right = right.astype(jnp.float32)
    gain = gain.reshape(1, channels)
    fixed = [right, gain, w_expand, w_contract]
    return pl.pallas_call(
        pair_kernel,
        grid=(rows // block,),
        in_specs=[
            pl.BlockSpec((block, columns, channels), lambda step: (step, 0, 0)),
            pl.BlockSpec((block, channels), lambda step: (step, 0)),
        ]
        + [whole(array) for array in fixed],
        out_specs=pl.BlockSpec((block, columns, channels), lambda step: (step, 0, 0)),
        out_shape=jax.ShapeDtypeStruct(table_part.shape, jnp.bfloat16),
        compiler_params=pltpu.CompilerParams(vmem_limit_bytes=48 << 20),
        name="pair",
    )(table_part, left, *fixed)


def first_norm_kernel(hidden_ref, gain_ref, out_ref):
    for start in range(0, hidden_ref.shape[0], 32):
        rows = slice(start, start + 32)
        values = hidden_ref[rows, :].astype(jnp.float32)
        out_ref[rows, :] = layer_norm(values, gain_ref[...]).astype(jnp.bfloat16)


def first_norm(hidden, gain):
    gain = gain.reshape(1, -1)
    return pl.pallas_call(
        first_norm_kernel,
        grid=(1,),
        in_specs=[whole(hidden), whole(gain)],
        out_specs=whole(hidden),
        out_shape=jax.ShapeDtypeStruct(hidden.shape, jnp.bfloat16),
        compiler_params=pltpu.CompilerParams(vmem_limit_bytes=8 << 20),
        name="first_norm",
    )(hidden, gain)


def half_sums_kernel(
    place_ref, parts_ref, stream_ref, own_ref, other_ref, mine_ref, sent_ref, blocks_ref
):
    near, core = place_ref[0], place_ref[2]
    rows, features = stream_ref.shape
    local_width = features // 4
    half_columns = own_ref.shape[1]
    resid = stream_ref[...].astype(jnp.float32)
    for part in range(parts_ref.shape[0]):
        resid += parts_ref[part].astype(jnp.float32)
    average = jnp.sum(resid, -1, keepdims=True) / features
    centred = resid - average
    spread = jnp.sum(centred * centred, -1, keepdims=True)
    centred = centred.astype(jnp.bfloat16)
    for block in range(4):
        blocks_ref[block, :rows, :] = centred[:, block * local_width : (block + 1) * local_width]
        blocks_ref[block, rows:, :] = jnp.ones((16, local_width), jnp.bfloat16)
    line = lax.broadcasted_iota(jnp.int32, (16, half_columns), 0)
    for ref, side in ((own_ref, core), (other_ref, 1 - core)):
        total = jnp.zeros((rows + 16, half_columns), jnp.float32)
        for position, shift in enumerate((0, 1, 3, 2)):
            total += jnp.dot(
                blocks_ref[near ^ shift],
                ref[position * local_width : (position + 1) * local_width, :],
                preferred_element_type=jnp.float32,
            )
        columns = pl.ds(pl.multiple_of(side * half_columns, half_columns), half_columns)
        mine_ref[:, columns] = total
        sums = total[rows:]
        high = sums.astype(jnp.bfloat16).astype(jnp.float32)
        sums = jnp.where(line == 0, high, jnp.where(line == 1, sums - high, 0.0))
        sent_ref[:rows, columns] = total[:rows].astype(jnp.bfloat16)
        sent_ref[rows:, columns] = sums.astype(jnp.bfloat16)
    lane = lax.broadcasted_iota(jnp.int32, (rows, 128), 1)
    width = half_columns * 2
    mine_ref[:rows, width:] = jnp.where(lane < 2, average, spread)
    mine_ref[rows:, width:] = jnp.zeros((16, 128), jnp.float32)
    high_average = average.astype(jnp.bfloat16).astype(jnp.float32)
    high_spread = spread.astype(jnp.bfloat16).astype(jnp.float32)
    terms = jnp.where(
        lane == 0,
        high_average,
        jnp.where(
            lane == 1,
            average - high_average,
            jnp.where(lane == 2, high_spread, spread - high_spread),
        ),
    )
    sent_ref[:rows, width:] = terms.astype(jnp.bfloat16)
    sent_ref[rows:, width:] = jnp.zeros((16, 128), jnp.bfloat16)


def half_sums(place, parts, hidden, own, other):
    rows, features = parts.shape[1:]
    width = own.shape[1] * 2 + 128

    def fixed(array):
        return pl.BlockSpec(array.shape, lambda step, place: (0,) * array.ndim)

    spec = pl.BlockSpec((rows + 16, width), lambda step, place: (0, 0))
    return pl.pallas_call(
        half_sums_kernel,
        grid_spec=pltpu.PrefetchScalarGridSpec(
            num_scalar_prefetch=1,
            grid=(1,),
            in_specs=[
                fixed(parts),
                pl.BlockSpec((rows, features), lambda step, place: (place[0], place[1])),
                fixed(own),
                fixed(other),
            ],
            out_specs=[spec, spec],
            scratch_shapes=[pltpu.VMEM((4, rows + 16, features // 4), jnp.bfloat16)],
        ),
        out_shape=[
            jax.ShapeDtypeStruct((rows + 16, width), jnp.float32),
            jax.ShapeDtypeStruct((rows + 16, width), jnp.bfloat16),
        ],
        compiler_params=pltpu.CompilerParams(vmem_limit_bytes=24 << 20),
        name="half_sums",
    )(place, parts, hidden, own, other)


def local(
    hidden,
    rel_bins,
    attn_gain,
    w_query,
    w_key,
    w_value,
    w_out,
    final_gain,
    w_single,
    w_second,
    w_left,
    w_right,
    rel_table,
    pair_gain,
    w_expand,
    w_contract,
):
    row_count = hidden.shape[0]
    model_width = hidden.shape[1]
    local_width = w_query.shape[1]
    local_heads = local_width // HD
    positions = lax.axis_index("row") * row_count + jnp.arange(row_count, dtype=jnp.int32)
    core = lax.rem(lax.axis_index("row"), 2)
    col_index = lax.axis_index("col")
    half_columns = w_single.shape[1] // 2
    own_part = lax.dynamic_slice_in_dim(w_single, core * half_columns, half_columns, 1)
    own_part = (own_part.astype(jnp.float32) * final_gain[:, None]).astype(jnp.bfloat16)
    own_part, hidden = lax.optimization_barrier((own_part, hidden))
    quarter = [own_part] + [lax.ppermute(own_part, "col", flip_pairs(8, bit)) for bit in (1, 3, 2)]
    quarter = jnp.concatenate(quarter, 0)
    quarter_other = lax.ppermute(quarter, "row", flip_pairs(16, 1))

    attn_in = first_norm(hidden, attn_gain)
    keys = jnp.dot(attn_in, w_key, preferred_element_type=jnp.float32)
    keys = rotary(keys.reshape(row_count, local_heads, HD), positions).astype(jnp.bfloat16)
    values = jnp.dot(attn_in, w_value, preferred_element_type=jnp.float32).astype(jnp.bfloat16)
    stacked = jnp.concatenate([keys.reshape(row_count, local_width), values], 1)
    stacked, attn_in = lax.optimization_barrier((stacked, attn_in))

    blocks = [stacked] + [lax.ppermute(stacked, "row", flip_pairs(16, 2 * bit)) for bit in (1, 3, 2)]
    query = jnp.dot(attn_in, w_query, preferred_element_type=jnp.float32) * HD ** (-0.5)
    query = rotary(query.reshape(row_count, local_heads, HD), positions).astype(jnp.bfloat16)
    query = query.reshape(row_count, local_width)
    query, rel_bins = lax.optimization_barrier((query, rel_bins))
    other_query = lax.ppermute(query, "row", flip_pairs(16, 8))

    bin_codes = jnp.arange(rel_table.shape[0], dtype=jnp.int32)
    one_hot = (rel_bins[..., None] == bin_codes).astype(jnp.bfloat16)
    table_part = jnp.einsum(
        "ijb,bc->ijc", one_hot, rel_table, preferred_element_type=jnp.float32
    ).astype(jnp.bfloat16)

    own_half = jnp.concatenate(blocks, 0)
    other_half = lax.ppermute(own_half, "row", flip_pairs(16, 1))
    incoming = jnp.concatenate([own_half, other_half], 0)
    both_query = jnp.concatenate([query, other_query], 0).reshape(-1, local_heads, HD)
    key_block = incoming[:, :local_width].reshape(-1, local_heads, HD)
    value_block = incoming[:, local_width:].reshape(-1, local_heads, HD)
    scores = jnp.einsum("qhd,khd->hqk", both_query, key_block, preferred_element_type=jnp.float32)
    weights = jnp.exp(scores)
    totals = jnp.sum(weights, -1)
    numerator = jnp.einsum(
        "hqk,khd->hqd",
        weights.astype(jnp.bfloat16),
        value_block,
        preferred_element_type=jnp.float32,
    )
    sent_totals = jnp.transpose(totals[:, row_count:])
    high = lax.reduce_precision(sent_totals, 8, 7)
    sent = jnp.concatenate(
        [
            jnp.transpose(numerator[:, row_count:], (1, 0, 2)).reshape(row_count, local_width),
            jnp.pad(high, ((0, 0), (0, 32 - local_heads))),
            jnp.pad(sent_totals - high, ((0, 0), (0, 32 - local_heads))),
        ],
        1,
    ).astype(jnp.bfloat16)
    received = lax.ppermute(sent, "row", flip_pairs(16, 8)).astype(jnp.float32)
    other_totals = received[:, local_width : local_width + local_heads]
    other_totals += received[:, local_width + 32 : local_width + 32 + local_heads]
    totals = jnp.transpose(totals[:, :row_count]) + other_totals
    numerator = jnp.transpose(numerator[:, :row_count], (1, 0, 2))
    numerator += received[:, :local_width].reshape(row_count, local_heads, HD)
    context = (numerator / totals[..., None]).astype(jnp.bfloat16).reshape(row_count, local_width)
    half_width = model_width // 2
    attn_part = jnp.einsum(
        "rk,kxn->xrn",
        context,
        w_out.reshape(local_width, 2, half_width),
        preferred_element_type=jnp.float32,
    ).astype(jnp.bfloat16)

    own_count = row_count // 4
    far, near = col_index // 4, lax.rem(col_index, 4)
    parts = lax.all_to_all(
        attn_part.reshape(8, own_count, half_width), "col", 0, 0, tiled=False
    )
    parts, table_part = lax.optimization_barrier((parts, table_part))
    place = jnp.stack([near, far, core]).astype(jnp.int32)
    mine, sent = half_sums(place, parts, hidden, quarter, quarter_other)
    theirs = lax.ppermute(sent, "col", flip_pairs(8, 4)).astype(jnp.float32)
    width = half_columns * 2
    other_average = theirs[:own_count, width : width + 1] + theirs[:own_count, width + 1 : width + 2]
    other_spread = theirs[:own_count, width + 2 : width + 3] + theirs[:own_count, width + 3 : width + 4]
    average, spread = mine[:own_count, width : width + 1], mine[:own_count, width + 2 : width + 3]
    apart = 0.5 * (average - other_average)
    variance = (spread + other_spread + model_width * apart * apart) / model_width
    column_sums = mine[own_count : own_count + 1, :width] - (
        theirs[own_count : own_count + 1, :width] + theirs[own_count + 1 : own_count + 2, :width]
    )
    summed = mine[:own_count, :width] + theirs[:own_count, :width] + apart * column_sums
    lifted = jnp.maximum(summed * lax.rsqrt(variance + epsilon), 0.0).astype(jnp.bfloat16)
    single = jnp.dot(lifted, w_second, preferred_element_type=jnp.float32).astype(jnp.bfloat16)
    both = jnp.concatenate([w_left, w_right], 1)
    both = jnp.dot(single, both, preferred_element_type=jnp.float32).astype(jnp.bfloat16)
    both = lax.all_to_all(
        jnp.broadcast_to(both, (4,) + both.shape),
        "col",
        0,
        0,
        tiled=False,
        axis_index_groups=[[0, 1, 2, 3], [4, 5, 6, 7]],
    ).reshape(row_count, -1)
    channels = w_left.shape[1]
    left, right = both[:, :channels], both[:, channels:]
    pairs = right_pairs(lax.axis_size("row"), lax.axis_size("col"))
    own_right = lax.ppermute(right, ("row", "col"), pairs)
    other_right = lax.ppermute(own_right, "row", flip_pairs(16, 1))
    low = core == 0
    column_right = jnp.concatenate(
        [jnp.where(low, own_right, other_right), jnp.where(low, other_right, own_right)], 0
    )
    return pair_stage(table_part, left, column_right, pair_gain, w_expand, w_contract)


def solution(mesh):
    in_specs = (
        P("row", None),
        P("row", "col"),
        P(),
        P(None, "col"),
        P(None, "col"),
        P(None, "col"),
        P("col", None),
        P("col"),
        P("col", None),
        P(),
        P(),
        P(),
        P(),
        P(),
        P(),
        P(),
    )
    out_specs = P("row", "col", None)
    return jax.shard_map(local, mesh=mesh, in_specs=in_specs, out_specs=out_specs, check_vma=False)
```

```python
import math

import jax
import jax.numpy as jnp
from jax import lax
from jax.experimental import pallas as pl
from jax.experimental.pallas import tpu as pltpu
from jax.sharding import PartitionSpec as P

HD = 64


epsilon = 1e-05


def layer_norm(values, gain):
    count = values.shape[-1]
    average = jnp.sum(values, -1, keepdims=True) / count
    variance = jnp.sum(values * values, -1, keepdims=True) / count - average * average
    return (values - average) * lax.rsqrt(variance + epsilon) * gain


def rotary(vectors, positions):
    half_size = vectors.shape[-1] // 2
    frequency = jnp.exp(
        jnp.arange(half_size, dtype=jnp.float32) * (-2.0 * math.log(10000.0) / vectors.shape[-1])
    )
    angles = positions.astype(jnp.float32)[:, None] * frequency[None, :]
    angles = jnp.concatenate([angles, angles], -1)[:, None, :]
    turned = jnp.concatenate([-vectors[..., half_size:], vectors[..., :half_size]], -1)
    return vectors * jnp.cos(angles) + turned * jnp.sin(angles)


def flip_pairs(size, bit):
    return [(place, place ^ bit) for place in range(size)]


def right_pairs(size, other_size):
    return [
        (
            (2 * col + row % 2) * other_size + row // 8 * 4 + (row // 2 + 2) % 4,
            row * other_size + col,
        )
        for row in range(size)
        for col in range(other_size)
    ]


def whole(array):
    return pl.BlockSpec(array.shape, lambda step: (0,) * array.ndim)


def pair_kernel(table_ref, left_ref, right_ref, gain_ref, expand_ref, contract_ref, out_ref):
    rows, columns, channels = table_ref.shape
    group = 8

    def pair_in(part):
        sums = left_ref[part, :][:, None, :] + right_ref[...][None]
        return table_ref[part].astype(jnp.float32) + sums

    for start in range(0, rows, group):
        part = slice(start, start + group)
        normed = layer_norm(pair_in(part), gain_ref[...]).astype(jnp.bfloat16)
        expanded = jnp.dot(
            normed.reshape(group * columns, channels),
            expand_ref[...],
            preferred_element_type=jnp.float32,
        )
        expanded = jnp.maximum(expanded.astype(jnp.bfloat16), 0)
        update = jnp.dot(expanded, contract_ref[...], preferred_element_type=jnp.float32)
        out_ref[part] = (pair_in(part) + update.reshape(group, columns, channels)).astype(
            jnp.bfloat16
        )


def pair_stage(table_part, left, right, gain, w_expand, w_contract):
    rows, columns, channels = table_part.shape
    block = 16
    left = left.astype(jnp.float32)
    right = right.astype(jnp.float32)
    gain = gain.reshape(1, channels)
    fixed = [right, gain, w_expand, w_contract]
    return pl.pallas_call(
        pair_kernel,
        grid=(rows // block,),
        in_specs=[
            pl.BlockSpec((block, columns, channels), lambda step: (step, 0, 0)),
            pl.BlockSpec((block, channels), lambda step: (step, 0)),
        ]
        + [whole(array) for array in fixed],
        out_specs=pl.BlockSpec((block, columns, channels), lambda step: (step, 0, 0)),
        out_shape=jax.ShapeDtypeStruct(table_part.shape, jnp.bfloat16),
        compiler_params=pltpu.CompilerParams(vmem_limit_bytes=24 << 20),
        name="pair",
    )(table_part, left, *fixed)


def first_norm_kernel(hidden_ref, gain_ref, out_ref):
    for start in range(0, hidden_ref.shape[0], 32):
        rows = slice(start, start + 32)
        values = hidden_ref[rows, :].astype(jnp.float32)
        out_ref[rows, :] = layer_norm(values, gain_ref[...][None, :]).astype(jnp.bfloat16)


def first_norm(hidden, gain):
    return pl.pallas_call(
        first_norm_kernel,
        grid=(1,),
        in_specs=[whole(hidden), whole(gain)],
        out_specs=whole(hidden),
        out_shape=jax.ShapeDtypeStruct(hidden.shape, jnp.bfloat16),
        compiler_params=pltpu.CompilerParams(vmem_limit_bytes=8 << 20),
        name="first_norm",
    )(hidden, gain)


def half_sums_kernel(
    place_ref, parts_ref, stream_ref, own_ref, other_ref, mine_ref, sent_ref, blocks_ref
):
    near, core = place_ref[0], place_ref[2]
    rows, features = stream_ref.shape
    local_width = features // 4
    half_columns = own_ref.shape[1]
    resid = stream_ref[...].astype(jnp.float32)
    for part in range(parts_ref.shape[0]):
        resid += parts_ref[part].astype(jnp.float32)
    average = jnp.sum(resid, -1, keepdims=True) / features
    centred = resid - average
    spread = jnp.sum(centred * centred, -1, keepdims=True)
    centred = centred.astype(jnp.bfloat16)
    for block in range(4):
        blocks_ref[block, :rows, :] = centred[:, block * local_width : (block + 1) * local_width]
        blocks_ref[block, rows:, :] = jnp.ones((16, local_width), jnp.bfloat16)
    line = lax.broadcasted_iota(jnp.int32, (16, half_columns), 0)
    for ref, side in ((own_ref, core), (other_ref, 1 - core)):
        total = jnp.zeros((rows + 16, half_columns), jnp.float32)
        for position, shift in enumerate((0, 1, 3, 2)):
            total += jnp.dot(
                blocks_ref[near ^ shift],
                ref[position * local_width : (position + 1) * local_width, :],
                preferred_element_type=jnp.float32,
            )
        columns = pl.ds(pl.multiple_of(side * half_columns, half_columns), half_columns)
        mine_ref[:, columns] = total
        sums = total[rows:]
        high = sums.astype(jnp.bfloat16).astype(jnp.float32)
        sums = jnp.where(line == 0, high, jnp.where(line == 1, sums - high, 0.0))
        sent_ref[:rows, columns] = total[:rows].astype(jnp.bfloat16)
        sent_ref[rows:, columns] = sums.astype(jnp.bfloat16)
    lane = lax.broadcasted_iota(jnp.int32, (rows, 128), 1)
    width = half_columns * 2
    mine_ref[:rows, width:] = jnp.where(lane < 2, average, spread)
    mine_ref[rows:, width:] = jnp.zeros((16, 128), jnp.float32)
    high_average = average.astype(jnp.bfloat16).astype(jnp.float32)
    high_spread = spread.astype(jnp.bfloat16).astype(jnp.float32)
    terms = jnp.where(
        lane == 0,
        high_average,
        jnp.where(
            lane == 1,
            average - high_average,
            jnp.where(lane == 2, high_spread, spread - high_spread),
        ),
    )
    sent_ref[:rows, width:] = terms.astype(jnp.bfloat16)
    sent_ref[rows:, width:] = jnp.zeros((16, 128), jnp.bfloat16)


def half_sums(place, parts, hidden, own, other):
    rows, features = parts.shape[1:]
    width = own.shape[1] * 2 + 128

    def fixed(array):
        return pl.BlockSpec(array.shape, lambda step, place: (0,) * array.ndim)

    spec = pl.BlockSpec((rows + 16, width), lambda step, place: (0, 0))
    return pl.pallas_call(
        half_sums_kernel,
        grid_spec=pltpu.PrefetchScalarGridSpec(
            num_scalar_prefetch=1,
            grid=(1,),
            in_specs=[
                fixed(parts),
                pl.BlockSpec((rows, features), lambda step, place: (place[0], place[1])),
                fixed(own),
                fixed(other),
            ],
            out_specs=[spec, spec],
            scratch_shapes=[pltpu.VMEM((4, rows + 16, features // 4), jnp.bfloat16)],
        ),
        out_shape=[
            jax.ShapeDtypeStruct((rows + 16, width), jnp.float32),
            jax.ShapeDtypeStruct((rows + 16, width), jnp.bfloat16),
        ],
        compiler_params=pltpu.CompilerParams(vmem_limit_bytes=24 << 20),
        name="half_sums",
    )(place, parts, hidden, own, other)


def local(
    hidden,
    rel_bins,
    attn_gain,
    w_query,
    w_key,
    w_value,
    w_out,
    final_gain,
    w_single,
    w_second,
    w_left,
    w_right,
    rel_table,
    pair_gain,
    w_expand,
    w_contract,
):
    row_count = hidden.shape[0]
    model_width = hidden.shape[1]
    local_width = w_query.shape[1]
    local_heads = local_width // HD
    positions = lax.axis_index("row") * row_count + jnp.arange(row_count, dtype=jnp.int32)
    core = lax.rem(lax.axis_index("row"), 2)
    col_index = lax.axis_index("col")
    attn_in = first_norm(hidden, attn_gain)
    keys = jnp.dot(attn_in, w_key, preferred_element_type=jnp.float32)
    keys = rotary(keys.reshape(row_count, local_heads, HD), positions).astype(jnp.bfloat16)
    values = jnp.dot(attn_in, w_value, preferred_element_type=jnp.float32).astype(jnp.bfloat16)
    stacked = jnp.concatenate([keys.reshape(row_count, local_width), values], 1)
    stacked, attn_in = lax.optimization_barrier((stacked, attn_in))

    blocks = [stacked] + [lax.ppermute(stacked, "row", flip_pairs(16, 2 * bit)) for bit in (1, 3, 2)]
    query = jnp.dot(attn_in, w_query, preferred_element_type=jnp.float32) * HD ** (-0.5)
    query = rotary(query.reshape(row_count, local_heads, HD), positions).astype(jnp.bfloat16)
    query = query.reshape(row_count, local_width)
    query, rel_bins = lax.optimization_barrier((query, rel_bins))
    other_query = lax.ppermute(query, "row", flip_pairs(16, 8))

    bin_codes = jnp.arange(rel_table.shape[0], dtype=jnp.int32)
    one_hot = (rel_bins[..., None] == bin_codes).astype(jnp.bfloat16)
    table_part = jnp.einsum(
        "ijb,bc->ijc", one_hot, rel_table, preferred_element_type=jnp.float32
    ).astype(jnp.bfloat16)

    own_half = jnp.concatenate(blocks, 0)
    other_half = lax.ppermute(own_half, "row", flip_pairs(16, 1))
    own_half, w_single = lax.optimization_barrier((own_half, w_single))
    half_columns = w_single.shape[1] // 2
    own_part = lax.dynamic_slice_in_dim(w_single, core * half_columns, half_columns, 1)
    own_part = (own_part.astype(jnp.float32) * final_gain[:, None]).astype(jnp.bfloat16)
    quarter = [own_part] + [lax.ppermute(own_part, "col", flip_pairs(8, bit)) for bit in (1, 3, 2)]
    quarter = jnp.concatenate(quarter, 0)
    quarter_other = lax.ppermute(quarter, "row", flip_pairs(16, 1))

    incoming = jnp.concatenate([own_half, other_half], 0)
    both_query = jnp.concatenate([query, other_query], 0).reshape(-1, local_heads, HD)
    key_block = incoming[:, :local_width].reshape(-1, local_heads, HD)
    value_block = incoming[:, local_width:].reshape(-1, local_heads, HD)
    scores = jnp.einsum("qhd,khd->hqk", both_query, key_block, preferred_element_type=jnp.float32)
    weights = jnp.exp(scores)
    totals = jnp.sum(weights, -1)
    numerator = jnp.einsum(
        "hqk,khd->hqd",
        weights.astype(jnp.bfloat16),
        value_block,
        preferred_element_type=jnp.float32,
    )
    sent_totals = jnp.transpose(totals[:, row_count:])
    high = lax.reduce_precision(sent_totals, 8, 7)
    sent = jnp.concatenate(
        [
            jnp.transpose(numerator[:, row_count:], (1, 0, 2)).reshape(row_count, local_width),
            jnp.pad(high, ((0, 0), (0, 32 - local_heads))),
            jnp.pad(sent_totals - high, ((0, 0), (0, 32 - local_heads))),
        ],
        1,
    ).astype(jnp.bfloat16)
    received = lax.ppermute(sent, "row", flip_pairs(16, 8)).astype(jnp.float32)
    other_totals = received[:, local_width : local_width + local_heads]
    other_totals += received[:, local_width + 32 : local_width + 32 + local_heads]
    totals = jnp.transpose(totals[:, :row_count]) + other_totals
    numerator = jnp.transpose(numerator[:, :row_count], (1, 0, 2))
    numerator += received[:, :local_width].reshape(row_count, local_heads, HD)
    context = (numerator / totals[..., None]).astype(jnp.bfloat16).reshape(row_count, local_width)
    half_width = model_width // 2
    attn_part = jnp.einsum(
        "rk,kxn->xrn",
        context,
        w_out.reshape(local_width, 2, half_width),
        preferred_element_type=jnp.float32,
    ).astype(jnp.bfloat16)

    own_count = row_count // 4
    far, near = col_index // 4, lax.rem(col_index, 4)
    parts = lax.all_to_all(
        attn_part.reshape(8, own_count, half_width), "col", 0, 0, tiled=False
    )
    parts, table_part = lax.optimization_barrier((parts, table_part))
    place = jnp.stack([near, far, core]).astype(jnp.int32)
    mine, sent = half_sums(place, parts, hidden, quarter, quarter_other)
    theirs = lax.ppermute(sent, "col", flip_pairs(8, 4)).astype(jnp.float32)
    width = half_columns * 2
    other_average = theirs[:own_count, width : width + 1] + theirs[:own_count, width + 1 : width + 2]
    other_spread = theirs[:own_count, width + 2 : width + 3] + theirs[:own_count, width + 3 : width + 4]
    average, spread = mine[:own_count, width : width + 1], mine[:own_count, width + 2 : width + 3]
    apart = 0.5 * (average - other_average)
    variance = (spread + other_spread + model_width * apart * apart) / model_width
    column_sums = mine[own_count : own_count + 1, :width] - (
        theirs[own_count : own_count + 1, :width] + theirs[own_count + 1 : own_count + 2, :width]
    )
    summed = mine[:own_count, :width] + theirs[:own_count, :width] + apart * column_sums
    lifted = jnp.maximum(summed * lax.rsqrt(variance + epsilon), 0.0).astype(jnp.bfloat16)
    single = jnp.dot(lifted, w_second, preferred_element_type=jnp.float32).astype(jnp.bfloat16)
    both = jnp.concatenate([w_left, w_right], 1)
    both = jnp.dot(single, both, preferred_element_type=jnp.float32).astype(jnp.bfloat16)
    both = lax.all_to_all(
        jnp.broadcast_to(both, (4,) + both.shape),
        "col",
        0,
        0,
        tiled=False,
        axis_index_groups=[[0, 1, 2, 3], [4, 5, 6, 7]],
    ).reshape(row_count, -1)
    channels = w_left.shape[1]
    left, right = both[:, :channels], both[:, channels:]
    pairs = right_pairs(lax.axis_size("row"), lax.axis_size("col"))
    own_right = lax.ppermute(right, ("row", "col"), pairs)
    other_right = lax.ppermute(own_right, "row", flip_pairs(16, 1))
    low = core == 0
    column_right = jnp.concatenate(
        [jnp.where(low, own_right, other_right), jnp.where(low, other_right, own_right)], 0
    )
    return pair_stage(table_part, left, column_right, pair_gain, w_expand, w_contract)


def solution(mesh):
    in_specs = (
        P("row", None),
        P("row", "col"),
        P(),
        P(None, "col"),
        P(None, "col"),
        P(None, "col"),
        P("col", None),
        P("col"),
        P("col", None),
        P(),
        P(),
        P(),
        P(),
        P(),
        P(),
        P(),
    )
    out_specs = P("row", "col", None)
    return jax.shard_map(local, mesh=mesh, in_specs=in_specs, out_specs=out_specs, check_vma=False)
```

```python
import math

import jax
import jax.numpy as jnp
from jax import lax
from jax.experimental import pallas as pl
from jax.experimental.pallas import tpu as pltpu
from jax.sharding import PartitionSpec as P

HD = 64


epsilon = 1e-05


def layer_norm(values, gain):
    count = values.shape[-1]
    average = jnp.sum(values, -1, keepdims=True) / count
    variance = jnp.sum(values * values, -1, keepdims=True) / count - average * average
    return (values - average) * lax.rsqrt(variance + epsilon) * gain


def rotary(vectors, positions):
    half_size = vectors.shape[-1] // 2
    frequency = jnp.exp(
        jnp.arange(half_size, dtype=jnp.float32) * (-2.0 * math.log(10000.0) / vectors.shape[-1])
    )
    angles = positions.astype(jnp.float32)[:, None] * frequency[None, :]
    angles = jnp.concatenate([angles, angles], -1)[:, None, :]
    turned = jnp.concatenate([-vectors[..., half_size:], vectors[..., :half_size]], -1)
    return vectors * jnp.cos(angles) + turned * jnp.sin(angles)


def flip_pairs(size, bit):
    return [(place, place ^ bit) for place in range(size)]


def right_pairs(size, other_size):
    return [
        (
            (2 * col + row % 2) * other_size + row // 8 * 4 + (row // 2 + 2) % 4,
            row * other_size + col,
        )
        for row in range(size)
        for col in range(other_size)
    ]


def whole(array):
    return pl.BlockSpec(array.shape, lambda step: (0,) * array.ndim)


def pair_kernel(table_ref, left_ref, right_ref, gain_ref, expand_ref, contract_ref, out_ref):
    rows, columns, channels = table_ref.shape
    group = 8

    def pair_in(part):
        sums = left_ref[part, :][:, None, :] + right_ref[...][None]
        return table_ref[part].astype(jnp.float32) + sums

    for start in range(0, rows, group):
        part = slice(start, start + group)
        normed = layer_norm(pair_in(part), gain_ref[...]).astype(jnp.bfloat16)
        expanded = jnp.dot(
            normed.reshape(group * columns, channels),
            expand_ref[...],
            preferred_element_type=jnp.float32,
        )
        expanded = jnp.maximum(expanded.astype(jnp.bfloat16), 0)
        update = jnp.dot(expanded, contract_ref[...], preferred_element_type=jnp.float32)
        out_ref[part] = (pair_in(part) + update.reshape(group, columns, channels)).astype(
            jnp.bfloat16
        )


def pair_stage(table_part, left, right, gain, w_expand, w_contract):
    rows, columns, channels = table_part.shape
    block = 16
    left = left.astype(jnp.float32)
    right = right.astype(jnp.float32)
    gain = gain.reshape(1, channels)
    fixed = [right, gain, w_expand, w_contract]
    return pl.pallas_call(
        pair_kernel,
        grid=(rows // block,),
        in_specs=[
            pl.BlockSpec((block, columns, channels), lambda step: (step, 0, 0)),
            pl.BlockSpec((block, channels), lambda step: (step, 0)),
        ]
        + [whole(array) for array in fixed],
        out_specs=pl.BlockSpec((block, columns, channels), lambda step: (step, 0, 0)),
        out_shape=jax.ShapeDtypeStruct(table_part.shape, jnp.bfloat16),
        compiler_params=pltpu.CompilerParams(vmem_limit_bytes=48 << 20),
        name="pair",
    )(table_part, left, *fixed)


def first_norm_kernel(hidden_ref, gain_ref, out_ref):
    for start in range(0, hidden_ref.shape[0], 32):
        rows = slice(start, start + 32)
        values = hidden_ref[rows, :].astype(jnp.float32)
        out_ref[rows, :] = layer_norm(values, gain_ref[...][None, :]).astype(jnp.bfloat16)


def first_norm(hidden, gain):
    return pl.pallas_call(
        first_norm_kernel,
        grid=(1,),
        in_specs=[whole(hidden), whole(gain)],
        out_specs=whole(hidden),
        out_shape=jax.ShapeDtypeStruct(hidden.shape, jnp.bfloat16),
        compiler_params=pltpu.CompilerParams(vmem_limit_bytes=8 << 20),
        name="first_norm",
    )(hidden, gain)


def half_sums_kernel(
    place_ref, parts_ref, stream_ref, own_ref, other_ref, mine_ref, sent_ref, blocks_ref
):
    near, core = place_ref[0], place_ref[2]
    rows, features = stream_ref.shape
    local_width = features // 4
    half_columns = own_ref.shape[1]
    resid = stream_ref[...].astype(jnp.float32)
    for part in range(parts_ref.shape[0]):
        resid += parts_ref[part].astype(jnp.float32)
    average = jnp.sum(resid, -1, keepdims=True) / features
    centred = resid - average
    spread = jnp.sum(centred * centred, -1, keepdims=True)
    centred = centred.astype(jnp.bfloat16)
    for block in range(4):
        blocks_ref[block, :rows, :] = centred[:, block * local_width : (block + 1) * local_width]
        blocks_ref[block, rows:, :] = jnp.ones((16, local_width), jnp.bfloat16)
    line = lax.broadcasted_iota(jnp.int32, (16, half_columns), 0)
    for ref, side in ((own_ref, core), (other_ref, 1 - core)):
        total = jnp.zeros((rows + 16, half_columns), jnp.float32)
        for position, shift in enumerate((0, 1, 3, 2)):
            total += jnp.dot(
                blocks_ref[near ^ shift],
                ref[position * local_width : (position + 1) * local_width, :],
                preferred_element_type=jnp.float32,
            )
        columns = pl.ds(pl.multiple_of(side * half_columns, half_columns), half_columns)
        mine_ref[:, columns] = total
        sums = total[rows:]
        high = sums.astype(jnp.bfloat16).astype(jnp.float32)
        sums = jnp.where(line == 0, high, jnp.where(line == 1, sums - high, 0.0))
        sent_ref[:rows, columns] = total[:rows].astype(jnp.bfloat16)
        sent_ref[rows:, columns] = sums.astype(jnp.bfloat16)
    lane = lax.broadcasted_iota(jnp.int32, (rows, 128), 1)
    width = half_columns * 2
    mine_ref[:rows, width:] = jnp.where(lane < 2, average, spread)
    mine_ref[rows:, width:] = jnp.zeros((16, 128), jnp.float32)
    high_average = average.astype(jnp.bfloat16).astype(jnp.float32)
    high_spread = spread.astype(jnp.bfloat16).astype(jnp.float32)
    terms = jnp.where(
        lane == 0,
        high_average,
        jnp.where(
            lane == 1,
            average - high_average,
            jnp.where(lane == 2, high_spread, spread - high_spread),
        ),
    )
    sent_ref[:rows, width:] = terms.astype(jnp.bfloat16)
    sent_ref[rows:, width:] = jnp.zeros((16, 128), jnp.bfloat16)


def half_sums(place, parts, hidden, own, other):
    rows, features = parts.shape[1:]
    width = own.shape[1] * 2 + 128

    def fixed(array):
        return pl.BlockSpec(array.shape, lambda step, place: (0,) * array.ndim)

    spec = pl.BlockSpec((rows + 16, width), lambda step, place: (0, 0))
    return pl.pallas_call(
        half_sums_kernel,
        grid_spec=pltpu.PrefetchScalarGridSpec(
            num_scalar_prefetch=1,
            grid=(1,),
            in_specs=[
                fixed(parts),
                pl.BlockSpec((rows, features), lambda step, place: (place[0], place[1])),
                fixed(own),
                fixed(other),
            ],
            out_specs=[spec, spec],
            scratch_shapes=[pltpu.VMEM((4, rows + 16, features // 4), jnp.bfloat16)],
        ),
        out_shape=[
            jax.ShapeDtypeStruct((rows + 16, width), jnp.float32),
            jax.ShapeDtypeStruct((rows + 16, width), jnp.bfloat16),
        ],
        compiler_params=pltpu.CompilerParams(vmem_limit_bytes=24 << 20),
        name="half_sums",
    )(place, parts, hidden, own, other)


def local(
    hidden,
    rel_bins,
    attn_gain,
    w_query,
    w_key,
    w_value,
    w_out,
    final_gain,
    w_single,
    w_second,
    w_left,
    w_right,
    rel_table,
    pair_gain,
    w_expand,
    w_contract,
):
    row_count = hidden.shape[0]
    model_width = hidden.shape[1]
    local_width = w_query.shape[1]
    local_heads = local_width // HD
    positions = lax.axis_index("row") * row_count + jnp.arange(row_count, dtype=jnp.int32)
    core = lax.rem(lax.axis_index("row"), 2)
    col_index = lax.axis_index("col")
    half_columns = w_single.shape[1] // 2
    own_part = lax.dynamic_slice_in_dim(w_single, core * half_columns, half_columns, 1)
    own_part = (own_part.astype(jnp.float32) * final_gain[:, None]).astype(jnp.bfloat16)
    own_part, hidden = lax.optimization_barrier((own_part, hidden))
    quarter = [own_part] + [lax.ppermute(own_part, "col", flip_pairs(8, bit)) for bit in (1, 3, 2)]
    quarter = jnp.concatenate(quarter, 0)
    quarter_other = lax.ppermute(quarter, "row", flip_pairs(16, 1))

    attn_in = first_norm(hidden, attn_gain)
    keys = jnp.dot(attn_in, w_key, preferred_element_type=jnp.float32)
    keys = rotary(keys.reshape(row_count, local_heads, HD), positions).astype(jnp.bfloat16)
    values = jnp.dot(attn_in, w_value, preferred_element_type=jnp.float32).astype(jnp.bfloat16)
    stacked = jnp.concatenate([keys.reshape(row_count, local_width), values], 1)
    stacked, attn_in = lax.optimization_barrier((stacked, attn_in))

    blocks = [stacked] + [lax.ppermute(stacked, "row", flip_pairs(16, 2 * bit)) for bit in (1, 3, 2)]
    query = jnp.dot(attn_in, w_query, preferred_element_type=jnp.float32) * HD ** (-0.5)
    query = rotary(query.reshape(row_count, local_heads, HD), positions).astype(jnp.bfloat16)
    query = query.reshape(row_count, local_width)
    query, rel_bins = lax.optimization_barrier((query, rel_bins))
    other_query = lax.ppermute(query, "row", flip_pairs(16, 8))

    bin_codes = jnp.arange(rel_table.shape[0], dtype=jnp.int32)
    one_hot = (rel_bins[..., None] == bin_codes).astype(jnp.bfloat16)
    table_part = jnp.einsum(
        "ijb,bc->ijc", one_hot, rel_table, preferred_element_type=jnp.float32
    ).astype(jnp.bfloat16)

    own_half = jnp.concatenate(blocks, 0)
    other_half = lax.ppermute(own_half, "row", flip_pairs(16, 1))
    incoming = jnp.concatenate([own_half, other_half], 0)
    both_query = jnp.concatenate([query, other_query], 0).reshape(-1, local_heads, HD)
    key_block = incoming[:, :local_width].reshape(-1, local_heads, HD)
    value_block = incoming[:, local_width:].reshape(-1, local_heads, HD)
    scores = jnp.einsum("qhd,khd->hqk", both_query, key_block, preferred_element_type=jnp.float32)
    weights = jnp.exp(scores)
    totals = jnp.sum(weights, -1)
    numerator = jnp.einsum(
        "hqk,khd->hqd",
        weights.astype(jnp.bfloat16),
        value_block,
        preferred_element_type=jnp.float32,
    )
    sent_totals = jnp.transpose(totals[:, row_count:])
    high = lax.reduce_precision(sent_totals, 8, 7)
    sent = jnp.concatenate(
        [
            jnp.transpose(numerator[:, row_count:], (1, 0, 2)).reshape(row_count, local_width),
            jnp.pad(high, ((0, 0), (0, 32 - local_heads))),
            jnp.pad(sent_totals - high, ((0, 0), (0, 32 - local_heads))),
        ],
        1,
    ).astype(jnp.bfloat16)
    received = lax.ppermute(sent, "row", flip_pairs(16, 8)).astype(jnp.float32)
    other_totals = received[:, local_width : local_width + local_heads]
    other_totals += received[:, local_width + 32 : local_width + 32 + local_heads]
    totals = jnp.transpose(totals[:, :row_count]) + other_totals
    numerator = jnp.transpose(numerator[:, :row_count], (1, 0, 2))
    numerator += received[:, :local_width].reshape(row_count, local_heads, HD)
    context = (numerator / totals[..., None]).astype(jnp.bfloat16).reshape(row_count, local_width)
    half_width = model_width // 2
    attn_part = jnp.einsum(
        "rk,kxn->xrn",
        context,
        w_out.reshape(local_width, 2, half_width),
        preferred_element_type=jnp.float32,
    ).astype(jnp.bfloat16)

    own_count = row_count // 4
    far, near = col_index // 4, lax.rem(col_index, 4)
    parts = lax.all_to_all(
        attn_part.reshape(8, own_count, half_width), "col", 0, 0, tiled=False
    )
    parts, table_part = lax.optimization_barrier((parts, table_part))
    place = jnp.stack([near, far, core]).astype(jnp.int32)
    mine, sent = half_sums(place, parts, hidden, quarter, quarter_other)
    theirs = lax.ppermute(sent, "col", flip_pairs(8, 4)).astype(jnp.float32)
    width = half_columns * 2
    other_average = theirs[:own_count, width : width + 1] + theirs[:own_count, width + 1 : width + 2]
    other_spread = theirs[:own_count, width + 2 : width + 3] + theirs[:own_count, width + 3 : width + 4]
    average, spread = mine[:own_count, width : width + 1], mine[:own_count, width + 2 : width + 3]
    apart = 0.5 * (average - other_average)
    variance = (spread + other_spread + model_width * apart * apart) / model_width
    column_sums = mine[own_count : own_count + 1, :width] - (
        theirs[own_count : own_count + 1, :width] + theirs[own_count + 1 : own_count + 2, :width]
    )
    summed = mine[:own_count, :width] + theirs[:own_count, :width] + apart * column_sums
    lifted = jnp.maximum(summed * lax.rsqrt(variance + epsilon), 0.0).astype(jnp.bfloat16)
    single = jnp.dot(lifted, w_second, preferred_element_type=jnp.float32).astype(jnp.bfloat16)
    both = jnp.concatenate([w_left, w_right], 1)
    both = jnp.dot(single, both, preferred_element_type=jnp.float32).astype(jnp.bfloat16)
    both = lax.all_to_all(
        jnp.broadcast_to(both, (4,) + both.shape),
        "col",
        0,
        0,
        tiled=False,
        axis_index_groups=[[0, 1, 2, 3], [4, 5, 6, 7]],
    ).reshape(row_count, -1)
    channels = w_left.shape[1]
    left, right = both[:, :channels], both[:, channels:]
    pairs = right_pairs(lax.axis_size("row"), lax.axis_size("col"))
    own_right = lax.ppermute(right, ("row", "col"), pairs)
    other_right = lax.ppermute(own_right, "row", flip_pairs(16, 1))
    low = core == 0
    column_right = jnp.concatenate(
        [jnp.where(low, own_right, other_right), jnp.where(low, other_right, own_right)], 0
    )
    return pair_stage(table_part, left, column_right, pair_gain, w_expand, w_contract)


def solution(mesh):
    in_specs = (
        P("row", None),
        P("row", "col"),
        P(),
        P(None, "col"),
        P(None, "col"),
        P(None, "col"),
        P("col", None),
        P("col"),
        P("col", None),
        P(),
        P(),
        P(),
        P(),
        P(),
        P(),
        P(),
    )
    out_specs = P("row", "col", None)
    return jax.shard_map(local, mesh=mesh, in_specs=in_specs, out_specs=out_specs, check_vma=False)
```

```python
import math

import jax
import jax.numpy as jnp
from jax import lax
from jax.experimental import pallas as pl
from jax.experimental.pallas import tpu as pltpu
from jax.sharding import PartitionSpec as P

HD = 64


epsilon = 1e-05


def layer_norm(values, gain):
    count = values.shape[-1]
    average = jnp.sum(values, -1, keepdims=True) / count
    variance = jnp.sum(values * values, -1, keepdims=True) / count - average * average
    return (values - average) * lax.rsqrt(variance + epsilon) * gain


def rotary(vectors, positions):
    half_size = vectors.shape[-1] // 2
    frequency = jnp.exp(
        jnp.arange(half_size, dtype=jnp.float32) * (-2.0 * math.log(10000.0) / vectors.shape[-1])
    )
    angles = positions.astype(jnp.float32)[:, None] * frequency[None, :]
    angles = jnp.concatenate([angles, angles], -1)[:, None, :]
    turned = jnp.concatenate([-vectors[..., half_size:], vectors[..., :half_size]], -1)
    return vectors * jnp.cos(angles) + turned * jnp.sin(angles)


def flip_pairs(size, bit):
    return [(place, place ^ bit) for place in range(size)]


def right_pairs(size, other_size):
    return [
        (
            (2 * col + row % 2) * other_size + row // 8 * 4 + (row // 2 + 2) % 4,
            row * other_size + col,
        )
        for row in range(size)
        for col in range(other_size)
    ]


def whole(array):
    return pl.BlockSpec(array.shape, lambda step: (0,) * array.ndim)


def pair_kernel(table_ref, left_ref, right_ref, gain_ref, expand_ref, contract_ref, out_ref):
    rows, columns, channels = table_ref.shape
    group = 16

    def pair_in(part):
        sums = left_ref[part, :][:, None, :] + right_ref[...][None]
        return table_ref[part].astype(jnp.float32) + sums

    for start in range(0, rows, group):
        part = slice(start, start + group)
        normed = layer_norm(pair_in(part), gain_ref[...]).astype(jnp.bfloat16)
        expanded = jnp.dot(
            normed.reshape(group * columns, channels),
            expand_ref[...],
            preferred_element_type=jnp.float32,
        )
        expanded = jnp.maximum(expanded.astype(jnp.bfloat16), 0)
        update = jnp.dot(expanded, contract_ref[...], preferred_element_type=jnp.float32)
        out_ref[part] = (pair_in(part) + update.reshape(group, columns, channels)).astype(
            jnp.bfloat16
        )


def pair_stage(table_part, left, right, gain, w_expand, w_contract):
    rows, columns, channels = table_part.shape
    block = 32
    left = left.astype(jnp.float32)
    right = right.astype(jnp.float32)
    gain = gain.reshape(1, channels)
    fixed = [right, gain, w_expand, w_contract]
    return pl.pallas_call(
        pair_kernel,
        grid=(rows // block,),
        in_specs=[
            pl.BlockSpec((block, columns, channels), lambda step: (step, 0, 0)),
            pl.BlockSpec((block, channels), lambda step: (step, 0)),
        ]
        + [whole(array) for array in fixed],
        out_specs=pl.BlockSpec((block, columns, channels), lambda step: (step, 0, 0)),
        out_shape=jax.ShapeDtypeStruct(table_part.shape, jnp.bfloat16),
        compiler_params=pltpu.CompilerParams(vmem_limit_bytes=48 << 20),
        name="pair",
    )(table_part, left, *fixed)


def first_norm_kernel(hidden_ref, gain_ref, out_ref):
    for start in range(0, hidden_ref.shape[0], 32):
        rows = slice(start, start + 32)
        values = hidden_ref[rows, :].astype(jnp.float32)
        out_ref[rows, :] = layer_norm(values, gain_ref[...][None, :]).astype(jnp.bfloat16)


def first_norm(hidden, gain):
    return pl.pallas_call(
        first_norm_kernel,
        grid=(1,),
        in_specs=[whole(hidden), whole(gain)],
        out_specs=whole(hidden),
        out_shape=jax.ShapeDtypeStruct(hidden.shape, jnp.bfloat16),
        compiler_params=pltpu.CompilerParams(vmem_limit_bytes=8 << 20),
        name="first_norm",
    )(hidden, gain)


def half_sums_kernel(
    place_ref, parts_ref, stream_ref, own_ref, other_ref, mine_ref, sent_ref, blocks_ref
):
    near, core = place_ref[0], place_ref[2]
    rows, features = stream_ref.shape
    local_width = features // 4
    half_columns = own_ref.shape[1]
    resid = stream_ref[...].astype(jnp.float32)
    for part in range(parts_ref.shape[0]):
        resid += parts_ref[part].astype(jnp.float32)
    average = jnp.sum(resid, -1, keepdims=True) / features
    centred = resid - average
    spread = jnp.sum(centred * centred, -1, keepdims=True)
    centred = centred.astype(jnp.bfloat16)
    for block in range(4):
        blocks_ref[block, :rows, :] = centred[:, block * local_width : (block + 1) * local_width]
        blocks_ref[block, rows:, :] = jnp.ones((16, local_width), jnp.bfloat16)
    line = lax.broadcasted_iota(jnp.int32, (16, half_columns), 0)
    for ref, side in ((own_ref, core), (other_ref, 1 - core)):
        total = jnp.zeros((rows + 16, half_columns), jnp.float32)
        for position, shift in enumerate((0, 1, 3, 2)):
            total += jnp.dot(
                blocks_ref[near ^ shift],
                ref[position * local_width : (position + 1) * local_width, :],
                preferred_element_type=jnp.float32,
            )
        columns = pl.ds(pl.multiple_of(side * half_columns, half_columns), half_columns)
        mine_ref[:, columns] = total
        sums = total[rows:]
        high = sums.astype(jnp.bfloat16).astype(jnp.float32)
        sums = jnp.where(line == 0, high, jnp.where(line == 1, sums - high, 0.0))
        sent_ref[:rows, columns] = total[:rows].astype(jnp.bfloat16)
        sent_ref[rows:, columns] = sums.astype(jnp.bfloat16)
    lane = lax.broadcasted_iota(jnp.int32, (rows, 128), 1)
    width = half_columns * 2
    mine_ref[:rows, width:] = jnp.where(lane < 2, average, spread)
    mine_ref[rows:, width:] = jnp.zeros((16, 128), jnp.float32)
    high_average = average.astype(jnp.bfloat16).astype(jnp.float32)
    high_spread = spread.astype(jnp.bfloat16).astype(jnp.float32)
    terms = jnp.where(
        lane == 0,
        high_average,
        jnp.where(
            lane == 1,
            average - high_average,
            jnp.where(lane == 2, high_spread, spread - high_spread),
        ),
    )
    sent_ref[:rows, width:] = terms.astype(jnp.bfloat16)
    sent_ref[rows:, width:] = jnp.zeros((16, 128), jnp.bfloat16)


def half_sums(place, parts, hidden, own, other):
    rows, features = parts.shape[1:]
    width = own.shape[1] * 2 + 128

    def fixed(array):
        return pl.BlockSpec(array.shape, lambda step, place: (0,) * array.ndim)

    spec = pl.BlockSpec((rows + 16, width), lambda step, place: (0, 0))
    return pl.pallas_call(
        half_sums_kernel,
        grid_spec=pltpu.PrefetchScalarGridSpec(
            num_scalar_prefetch=1,
            grid=(1,),
            in_specs=[
                fixed(parts),
                pl.BlockSpec((rows, features), lambda step, place: (place[0], place[1])),
                fixed(own),
                fixed(other),
            ],
            out_specs=[spec, spec],
            scratch_shapes=[pltpu.VMEM((4, rows + 16, features // 4), jnp.bfloat16)],
        ),
        out_shape=[
            jax.ShapeDtypeStruct((rows + 16, width), jnp.float32),
            jax.ShapeDtypeStruct((rows + 16, width), jnp.bfloat16),
        ],
        compiler_params=pltpu.CompilerParams(vmem_limit_bytes=24 << 20),
        name="half_sums",
    )(place, parts, hidden, own, other)


def local(
    hidden,
    rel_bins,
    attn_gain,
    w_query,
    w_key,
    w_value,
    w_out,
    final_gain,
    w_single,
    w_second,
    w_left,
    w_right,
    rel_table,
    pair_gain,
    w_expand,
    w_contract,
):
    row_count = hidden.shape[0]
    model_width = hidden.shape[1]
    local_width = w_query.shape[1]
    local_heads = local_width // HD
    positions = lax.axis_index("row") * row_count + jnp.arange(row_count, dtype=jnp.int32)
    core = lax.rem(lax.axis_index("row"), 2)
    col_index = lax.axis_index("col")
    half_columns = w_single.shape[1] // 2
    own_part = lax.dynamic_slice_in_dim(w_single, core * half_columns, half_columns, 1)
    own_part = (own_part.astype(jnp.float32) * final_gain[:, None]).astype(jnp.bfloat16)
    own_part, attn_gain = lax.optimization_barrier((own_part, attn_gain))
    quarter = [own_part] + [lax.ppermute(own_part, "col", flip_pairs(8, bit)) for bit in (1, 3, 2)]
    quarter = jnp.concatenate(quarter, 0)
    quarter_other = lax.ppermute(quarter, "row", flip_pairs(16, 1))

    attn_in = first_norm(hidden, attn_gain)
    keys = jnp.dot(attn_in, w_key, preferred_element_type=jnp.float32)
    keys = rotary(keys.reshape(row_count, local_heads, HD), positions).astype(jnp.bfloat16)
    values = jnp.dot(attn_in, w_value, preferred_element_type=jnp.float32).astype(jnp.bfloat16)
    stacked = jnp.concatenate([keys.reshape(row_count, local_width), values], 1)
    stacked, attn_in = lax.optimization_barrier((stacked, attn_in))

    blocks = [stacked] + [lax.ppermute(stacked, "row", flip_pairs(16, 2 * bit)) for bit in (1, 3, 2)]
    query = jnp.dot(attn_in, w_query, preferred_element_type=jnp.float32) * HD ** (-0.5)
    query = rotary(query.reshape(row_count, local_heads, HD), positions).astype(jnp.bfloat16)
    query = query.reshape(row_count, local_width)
    query, rel_bins = lax.optimization_barrier((query, rel_bins))
    other_query = lax.ppermute(query, "row", flip_pairs(16, 8))

    bin_codes = jnp.arange(rel_table.shape[0], dtype=jnp.int32)
    one_hot = (rel_bins[..., None] == bin_codes).astype(jnp.bfloat16)
    table_part = jnp.einsum(
        "ijb,bc->ijc", one_hot, rel_table, preferred_element_type=jnp.float32
    ).astype(jnp.bfloat16)

    own_half = jnp.concatenate(blocks, 0)
    other_half = lax.ppermute(own_half, "row", flip_pairs(16, 1))
    incoming = jnp.concatenate([own_half, other_half], 0)
    both_query = jnp.concatenate([query, other_query], 0).reshape(-1, local_heads, HD)
    key_block = incoming[:, :local_width].reshape(-1, local_heads, HD)
    value_block = incoming[:, local_width:].reshape(-1, local_heads, HD)
    scores = jnp.einsum("qhd,khd->hqk", both_query, key_block, preferred_element_type=jnp.float32)
    weights = jnp.exp(scores)
    totals = jnp.sum(weights, -1)
    numerator = jnp.einsum(
        "hqk,khd->hqd",
        weights.astype(jnp.bfloat16),
        value_block,
        preferred_element_type=jnp.float32,
    )
    sent_totals = jnp.transpose(totals[:, row_count:])
    high = lax.reduce_precision(sent_totals, 8, 7)
    sent = jnp.concatenate(
        [
            jnp.transpose(numerator[:, row_count:], (1, 0, 2)).reshape(row_count, local_width),
            jnp.pad(high, ((0, 0), (0, 32 - local_heads))),
            jnp.pad(sent_totals - high, ((0, 0), (0, 32 - local_heads))),
        ],
        1,
    ).astype(jnp.bfloat16)
    received = lax.ppermute(sent, "row", flip_pairs(16, 8)).astype(jnp.float32)
    other_totals = received[:, local_width : local_width + local_heads]
    other_totals += received[:, local_width + 32 : local_width + 32 + local_heads]
    totals = jnp.transpose(totals[:, :row_count]) + other_totals
    numerator = jnp.transpose(numerator[:, :row_count], (1, 0, 2))
    numerator += received[:, :local_width].reshape(row_count, local_heads, HD)
    context = (numerator / totals[..., None]).astype(jnp.bfloat16).reshape(row_count, local_width)
    half_width = model_width // 2
    attn_part = jnp.einsum(
        "rk,kxn->xrn",
        context,
        w_out.reshape(local_width, 2, half_width),
        preferred_element_type=jnp.float32,
    ).astype(jnp.bfloat16)

    own_count = row_count // 4
    far, near = col_index // 4, lax.rem(col_index, 4)
    parts = lax.all_to_all(
        attn_part.reshape(8, own_count, half_width), "col", 0, 0, tiled=False
    )
    parts, table_part = lax.optimization_barrier((parts, table_part))
    place = jnp.stack([near, far, core]).astype(jnp.int32)
    mine, sent = half_sums(place, parts, hidden, quarter, quarter_other)
    theirs = lax.ppermute(sent, "col", flip_pairs(8, 4)).astype(jnp.float32)
    width = half_columns * 2
    other_average = theirs[:own_count, width : width + 1] + theirs[:own_count, width + 1 : width + 2]
    other_spread = theirs[:own_count, width + 2 : width + 3] + theirs[:own_count, width + 3 : width + 4]
    average, spread = mine[:own_count, width : width + 1], mine[:own_count, width + 2 : width + 3]
    apart = 0.5 * (average - other_average)
    variance = (spread + other_spread + model_width * apart * apart) / model_width
    column_sums = mine[own_count : own_count + 1, :width] - (
        theirs[own_count : own_count + 1, :width] + theirs[own_count + 1 : own_count + 2, :width]
    )
    summed = mine[:own_count, :width] + theirs[:own_count, :width] + apart * column_sums
    lifted = jnp.maximum(summed * lax.rsqrt(variance + epsilon), 0.0).astype(jnp.bfloat16)
    single = jnp.dot(lifted, w_second, preferred_element_type=jnp.float32).astype(jnp.bfloat16)
    both = jnp.concatenate([w_left, w_right], 1)
    both = jnp.dot(single, both, preferred_element_type=jnp.float32).astype(jnp.bfloat16)
    both = lax.all_to_all(
        jnp.broadcast_to(both, (4,) + both.shape),
        "col",
        0,
        0,
        tiled=False,
        axis_index_groups=[[0, 1, 2, 3], [4, 5, 6, 7]],
    ).reshape(row_count, -1)
    channels = w_left.shape[1]
    left, right = both[:, :channels], both[:, channels:]
    pairs = right_pairs(lax.axis_size("row"), lax.axis_size("col"))
    own_right = lax.ppermute(right, ("row", "col"), pairs)
    other_right = lax.ppermute(own_right, "row", flip_pairs(16, 1))
    low = core == 0
    column_right = jnp.concatenate(
        [jnp.where(low, own_right, other_right), jnp.where(low, other_right, own_right)], 0
    )
    return pair_stage(table_part, left, column_right, pair_gain, w_expand, w_contract)


def solution(mesh):
    in_specs = (
        P("row", None),
        P("row", "col"),
        P(),
        P(None, "col"),
        P(None, "col"),
        P(None, "col"),
        P("col", None),
        P("col"),
        P("col", None),
        P(),
        P(),
        P(),
        P(),
        P(),
        P(),
        P(),
    )
    out_specs = P("row", "col", None)
    return jax.shard_map(local, mesh=mesh, in_specs=in_specs, out_specs=out_specs, check_vma=False)
```
